128 devices in a mesh: facet: 32 (over z, x_hi, y), vis: 4 (over x_lo, core).
Axes of the slice: x: 4 (x_hi: 2, x_lo: 2; x = x_hi * 2 + x_lo), y: 4, z: 4, core: 2. Of those that a mesh axis runs over, the one named last changes fastest.
Arguments:
- facet_image: float32 [2, 32768, 1024], P(None, ('facet', 'vis')), may hold values from -0.005859375 to 0.005859375
- contributions: int32 [4, 32, 8], P(None, 'facet'), may hold values from 0 to 31, as said below
- counts: int32 [4, 32], P('vis', 'facet'), may hold values from 1 to 512, as said below
- wplanes: int32 [4, 32, 512], P('vis', 'facet'), may hold values from 0 to 7
- kernel_offsets: int32 [2, 4, 32, 512, 128], P(None, 'vis', 'facet'), may hold values from 0 to 56
- kernel_frac: float32 [2, 4, 32, 512, 128], P(None, 'vis', 'facet'), may hold values from 0 to 1
- owners: int32 [4, 32, 512, 1], P('vis', 'facet'), may hold values from 0 to 3; in each aligned block of 512 rows (0 to 511, 512 to 1023, ..., all dimensions but the last counted through in order) at most 256 rows name the same one
Outputs:
- owned: float32 [4, 32, 4, 256, 256], P('vis', 'facet')
The draws below stay inside these ranges and needn't reach their ends.
Inputs may be any that keep to these rules, and one draw needn't show every extreme that they name: For each column c, the lists contributions[r, c] of its 4 subgrids together name every facet exactly once. `counts`: subgrid (0, 0) has all 512 rows live. `owners`: the rows of one subgrid name one owner at most 256 times, and some subgrid names an owner exactly 256 times.
All inputs are finite; a program needn't handle non-finite values.
Results may differ from the reference program's by a relative error of at most 0.0003.
Values sent between devices are 32-bit elements; how exact they have to be, the bound alone decides.
No kernel may reach another device: no remote copies, remote signals or barrier semaphores. Data moves between devices by JAX's collectives and lax.ppermute only.
A program may use at most 64 MiB of HBM per device.

```python
import math
import jax
import jax.numpy as jnp
import numpy as np
from jax import lax

FP = 1024
SUB = 64
CH = 128
NW = 8
USTEP = 129
VSTEP = 33
ROWS = 512
K = 8
NCOL = 32
IMG = 32768
CAP = 256
N_FACET = 32
N_VIS = 4


def draw_contributions(key, part):
    key = jax.random.fold_in(key, 13)
    column_keys = jax.random.split(key, NCOL)
    orders = jax.vmap(lambda one: jax.random.permutation(one, N_FACET))(column_keys)
    return orders.astype(jnp.int32).reshape(NCOL, N_VIS, K).transpose(1, 0, 2)


def draw_counts(key, part):
    key = jax.random.fold_in(key, 11)
    values = jax.random.randint(key, (N_VIS, NCOL), ROWS // 8 + 1, ROWS + 1, dtype=jnp.int32)
    return values.at[0, 0].set(ROWS)


def with_ends(result, key, low, top_value):
    index_at = [jax.random.randint(jax.random.fold_in(key, axis), (), 0, length) for axis, length in enumerate(result.shape)]
    main_axis = result.shape.index(max(result.shape))
    next_to = index_at[:main_axis] + [(index_at[main_axis] + 1) % result.shape[main_axis]] + index_at[main_axis + 1:]
    return result.at[tuple(index_at)].set(low).at[tuple(next_to)].set(top_value)


def levels(rng, extent, pieces, smallest, top_value):
    def one(dim, parts):
        draws = jax.random.uniform(jax.random.fold_in(jax.random.fold_in(rng, 6), dim), (parts,), jnp.float32, smallest / len(pieces), top_value / len(pieces))
        return jnp.repeat(jnp.exp(draws), extent[dim] // parts).reshape((-1,) + (1,) * (len(extent) - dim - 1))

    factor_of = one(*pieces[0])
    for cut in pieces[1:]:
        factor_of = factor_of * one(*cut)
    return factor_of


def routed_block(rng, own, number, rows, amount, top, most, slope):
    ranking = jax.random.permutation(rng, amount)
    packed, ordinary = portions_of(amount, rows * top, most, slope, True), portions_of(amount, rows * top, most, slope, False)
    places = jnp.arange(amount)

    def named(lengths, offset_by):
        used = int((lengths > 0).sum())
        fixed = max(1, used // 4)
        passed = fixed + (places - fixed + offset_by * (used - fixed)) % max(1, amount - fixed)
        return jnp.zeros((amount,), jnp.int32).at[ranking[jnp.where(places < fixed, places, passed)]].set(jnp.asarray(lengths, jnp.int32))

    lengths = jnp.where(number % 4 == 0, named(packed, number // 4), named(ordinary, number - number // 4 - 1))
    mixed = jax.random.permutation(jax.random.fold_in(own, 3), amount)
    source_of, receiver = mixed[0:amount // 2 * 2:2], mixed[1:amount // 2 * 2:2]
    margin = jnp.minimum(lengths[source_of] - 1, most - lengths[receiver]) // 2
    margin = jnp.where((source_of == ranking[0]) | (receiver == ranking[0]) | (lengths[receiver] == 0), 0, jnp.maximum(margin, 0))
    passed = jax.random.randint(jax.random.fold_in(own, 4), (amount // 2,), 0, 1 << 20) % (margin + 1)
    lengths = lengths.at[source_of].add(-passed).at[receiver].add(passed)
    items = jnp.searchsorted(jnp.cumsum(lengths), jnp.arange(rows * top), side="right").astype(jnp.int32)
    table = items.reshape(top, rows).T
    table = table[jax.random.permutation(jax.random.fold_in(own, 1), rows)]
    offset_by = jax.random.randint(jax.random.fold_in(own, 2), (rows, 1), 0, top)
    return jnp.take_along_axis(table, (jnp.arange(top)[None, :] + offset_by) % top, axis=1)


def portions_of(amount, total, bound, slope, full):
    weights = [(1 << 20) // math.isqrt(standing ** slope) + 1 for standing in range(1, amount + 1)]
    largest = bound if full else min(bound, max(-(-total // amount), total * weights[0] // sum(weights)))
    least = 1 if total - largest >= amount - 1 else 0
    given, surplus = [largest] + [least] * (amount - 1), total - largest - least * (amount - 1)
    while surplus > 0:
        candidates = [i for i in range(1, amount) if given[i] < largest] or [i for i in range(1, amount) if given[i] < bound]
        mass, budget = sum([weights[i] for i in candidates]), surplus
        for i in candidates:
            addition = min(bound - given[i], max(1, budget * weights[i] // mass), surplus)
            given[i] = given[i] + addition
            surplus = surplus - addition
    return np.array(given)


def normal_values(rng, extent, scale, reach, cuts=(), held_as=jnp.bfloat16):
    gain = levels(rng, extent, cuts, -0.22, 0.18) if cuts else 1.0
    result = jax.random.normal(rng, extent, jnp.float32) * scale * gain
    return jnp.minimum(jnp.maximum(result, -reach), reach).astype(held_as)


def setup_inputs(seed: int = 0) -> dict:
    key_list = jax.random.split(jax.random.key(seed), 8)
    facet_image = normal_values(key_list[0], (2, IMG, FP), (1.0 / FP), 0.005859375, ((1, 128),), jnp.float32)
    contributions = draw_contributions(jax.random.fold_in(key_list[7], 71), 0)
    counts = draw_counts(jax.random.fold_in(key_list[7], 71), 0)
    wplanes = with_ends(jax.random.randint(key_list[3], (N_VIS, NCOL, ROWS), 0, NW), jax.random.fold_in(key_list[3], 1), 0, NW - 1).astype(jnp.int32)
    kernel_offsets = with_ends(jax.random.randint(key_list[4], (2, N_VIS, NCOL, ROWS, CH), 0, SUB - 7), jax.random.fold_in(key_list[4], 1), 0, (SUB - 7) - 1).astype(jnp.int32)
    kernel_frac = jnp.clip(1.0 * jax.random.uniform(key_list[5], (2, N_VIS, NCOL, ROWS, CH), jnp.float32) ** levels(key_list[5], (2, N_VIS, NCOL, ROWS, CH), ((1, 4), (2, 32)), -0.2, 0.2), 0.0, 1.0)
    owners_keys = jax.random.split(jax.random.fold_in(key_list[6], 1), N_VIS * NCOL * ROWS // ROWS)
    owners_turns = jax.random.permutation(jax.random.fold_in(key_list[6], 3), N_VIS * NCOL * ROWS // ROWS)
    owners = jax.vmap(lambda own, number: routed_block(jax.random.fold_in(key_list[6], 2), own, number, ROWS, N_VIS, 1, CAP, 2))(owners_keys, owners_turns).reshape((N_VIS, NCOL, ROWS, 1))
    return dict(facet_image=facet_image, contributions=contributions, counts=counts, wplanes=wplanes, kernel_offsets=kernel_offsets, kernel_frac=kernel_frac, owners=owners)


HIGHEST = lax.Precision.HIGHEST

def phase(first, second, modulus):
    return 2.0 * math.pi / modulus * (first * second % modulus).astype(jnp.float32)

def column_tables(first_col, ncols, half, width, modulus):
    ypos = jnp.arange(width, dtype=jnp.int32)
    freq = (first_col * half + jnp.arange(ncols * half, dtype=jnp.int32)) * VSTEP % modulus
    theta = phase(ypos[:, None], freq[None, :], modulus).reshape(width, ncols, half)
    cosine = jnp.cos(theta)
    sine = jnp.sin(theta)
    return (jnp.concatenate([cosine, -sine], -1), jnp.concatenate([sine, cosine], -1))

def swap_halves(values, half):
    return jnp.concatenate([values[..., half:], -values[..., :half]], -1)

def screened_planes(grid, planes_count):
    half = grid.shape[0]
    cells = jnp.arange(half, dtype=jnp.int32) - half // 2
    radius = cells[:, None] * cells[:, None] + cells[None, :] * cells[None, :]
    wsteps = jnp.arange(planes_count, dtype=jnp.int32)
    theta = 2.0 * math.pi / (half * half) * (wsteps[:, None, None] * radius[None] % (half * half)).astype(jnp.float32)
    real_part = grid[:, :half]
    imag_part = grid[:, half:]
    hre = real_part[None] * jnp.cos(theta) - imag_part[None] * jnp.sin(theta)
    him = real_part[None] * jnp.sin(theta) + imag_part[None] * jnp.cos(theta)
    index = jnp.arange(half, dtype=jnp.int32)
    angle = 2.0 * math.pi / half * (index[:, None] * index[None, :] % half).astype(jnp.float32)
    dcos = jnp.cos(angle) / math.sqrt(half)
    dsin = jnp.sin(angle) / math.sqrt(half)
    xre = jnp.einsum('ap,jpq->jaq', dcos, hre, precision=HIGHEST) + jnp.einsum('ap,jpq->jaq', dsin, him, precision=HIGHEST)
    xim = jnp.einsum('ap,jpq->jaq', dcos, him, precision=HIGHEST) - jnp.einsum('ap,jpq->jaq', dsin, hre, precision=HIGHEST)
    yre = jnp.einsum('jaq,bq->jab', xre, dcos, precision=HIGHEST) + jnp.einsum('jaq,bq->jab', xim, dsin, precision=HIGHEST)
    yim = jnp.einsum('jaq,bq->jab', xim, dcos, precision=HIGHEST) - jnp.einsum('jaq,bq->jab', xre, dsin, precision=HIGHEST)
    return jnp.concatenate([yre, yim], -1)

def kernel_rows(offsets, frac, half):
    cells = jnp.arange(half, dtype=jnp.int32)
    steps = cells[None, None, :] - offsets[..., None]
    inside = (steps >= 0) & (steps < 8)
    shifted = (steps.astype(jnp.float32) - frac[..., None] - 3.5) / 1.6
    return jnp.where(inside, 0.5 * jnp.exp(-0.5 * shifted * shifted), jnp.float32(0.0))

def degrid(planes, wrow, offsets, frac):
    half = planes.shape[1]
    chosen = jnp.take(planes, wrow, axis=0)
    ukernel = kernel_rows(offsets[0], frac[0], half)
    vkernel = kernel_rows(offsets[1], frac[1], half)
    along_u = jnp.einsum('nca,nak->nck', ukernel, chosen, precision=HIGHEST)
    real_vis = lax.optimization_barrier(jnp.sum(along_u[..., :half] * vkernel, -1))
    imag_vis = lax.optimization_barrier(jnp.sum(along_u[..., half:] * vkernel, -1))
    return jnp.concatenate([real_vis, imag_vis], -1)

def route(values, owner, nowners, slots):
    hot = (owner[:, None] == jnp.arange(nowners, dtype=jnp.int32)[None, :]).astype(jnp.int32)
    rank = lax.optimization_barrier(jnp.sum((jnp.cumsum(hot, 0) - hot) * hot, 1))
    place = ((owner[:, None, None] == jnp.arange(nowners, dtype=jnp.int32)[None, :, None]) & (rank[:, None, None] == jnp.arange(slots, dtype=jnp.int32)[None, None, :])).astype(jnp.float32)
    return jnp.einsum('nos,nk->osk', place, values, precision=HIGHEST)

def reference(facet_image, contributions, counts, wplanes, kernel_offsets, kernel_frac, owners):
    modulus = FP * N_FACET
    tab_re, tab_im = column_tables(0, N_FACET, SUB, FP, modulus)
    weights = lax.optimization_barrier(jnp.sum((contributions[..., None] == jnp.arange(N_FACET, dtype=jnp.int32)).astype(jnp.float32), 2))
    row_weights = jnp.repeat(weights, SUB, axis=0)
    kfreq = jnp.arange(N_VIS * SUB, dtype=jnp.int32) * USTEP % modulus

    def facet_step(total, facet):
        piece = lax.dynamic_slice_in_dim(facet_image, (facet * FP).astype(jnp.int32), FP, 1)
        panel = jnp.einsum('xy,yck->xck', piece[0], tab_re, precision=HIGHEST) + jnp.einsum('xy,yck->xck', piece[1], tab_im, precision=HIGHEST)
        xpos = facet * FP + jnp.arange(FP, dtype=jnp.int32)
        theta = phase(kfreq[:, None], xpos[None, :], modulus)
        cpart = jnp.einsum('rx,xck->rck', jnp.cos(theta), panel, precision=HIGHEST)
        spart = jnp.einsum('rx,xck->rck', jnp.sin(theta), panel, precision=HIGHEST)
        contrib = cpart + swap_halves(spart, SUB)
        return (total + contrib * row_weights[:, :, facet][..., None], None)
    total0 = jnp.zeros((N_VIS * SUB, N_FACET, 2 * SUB), jnp.float32)
    total, _ = lax.scan(facet_step, total0, jnp.arange(N_FACET, dtype=jnp.int32))
    grids = total.reshape(N_VIS, SUB, N_FACET, 2 * SUB).transpose(0, 2, 1, 3).reshape(N_VIS * N_FACET, SUB, 2 * SUB)
    wrows = wplanes.reshape(N_VIS * N_FACET, ROWS)
    offs = jnp.moveaxis(kernel_offsets, 0, 2).reshape(N_VIS * N_FACET, 2, ROWS, CH)
    fracs = jnp.moveaxis(kernel_frac, 0, 2).reshape(N_VIS * N_FACET, 2, ROWS, CH)
    live_counts = counts.reshape(N_VIS * N_FACET)
    owner_rows = owners.reshape(N_VIS * N_FACET, ROWS)

    def one_subgrid(items):
        grid, wrow, offset, frac, count, owner = items
        planes = screened_planes(grid, NW)
        values = degrid(planes, wrow, offset, frac)
        live = (jnp.arange(ROWS, dtype=jnp.int32) < count)[:, None]
        values = jnp.where(live, values, jnp.float32(0.0))
        return route(values, owner, N_VIS, CAP)
    routed = lax.map(one_subgrid, (grids, wrows, offs, fracs, live_counts, owner_rows))
    routed = routed.reshape(N_VIS, N_FACET, N_VIS, CAP, 2 * CH)
    return routed.transpose(2, 1, 0, 3, 4)
```

```python
import functools
import math

import jax
import jax.numpy as jnp
import ml_dtypes
import numpy as np
from jax import lax
from jax.experimental import pallas as pl
from jax.experimental.pallas import tpu as pltpu
from jax.sharding import PartitionSpec as P

FP = 1024
SUB = 64
CH = 128
NW = 8
USTEP = 129
VSTEP = 33
ROWS = 512
K = 8
NCOL = 32
CAP = 256
N_FACET = 32
N_VIS = 4
MOD = FP * N_FACET
XROWS = FP // N_VIS
YBLK = 256
NY = FP // YBLK

F32 = jnp.float32
BF16 = jnp.bfloat16
HIGHEST = lax.Precision.HIGHEST
VMEM_LIMIT = 56 * 1024 * 1024


def turns(first, second, modulus):
    return 2.0 * math.pi * ((first * second) % modulus) / modulus


def split_np(values):
    high = values.astype(ml_dtypes.bfloat16)
    low = (values - high.astype(np.float64)).astype(ml_dtypes.bfloat16)
    return high, low


@functools.cache
def tables():
    freq = USTEP * np.arange(N_VIS * SUB, dtype=np.int64)
    theta = turns(freq[:, None], np.arange(XROWS, dtype=np.int64)[None, :], MOD).reshape(N_VIS, SUB, XROWS)
    ch, cl = split_np(np.cos(theta))
    sh, sl = split_np(np.sin(theta))
    xtab = np.concatenate([ch, sh, cl, sl], 1)

    xrot = np.zeros((N_FACET * N_VIS, 8, N_VIS * SUB), np.float32)
    for f in range(N_FACET):
        for v in range(N_VIS):
            order = row_order(v // 2, v % 2)
            rows = np.concatenate([freq[r * SUB : (r + 1) * SUB] for r in order])
            angle = turns(rows, f * FP + v * XROWS, MOD)
            xrot[f * N_VIS + v, 0] = np.cos(angle)
            xrot[f * N_VIS + v, 1] = np.sin(angle)

    m = np.arange(NCOL * SUB, dtype=np.int64)
    theta = turns(np.arange(YBLK, dtype=np.int64)[:, None], VSTEP * m[None, :], MOD).reshape(YBLK, NCOL // 2, 128)
    ytab = np.concatenate([np.cos(theta), np.sin(theta)], -1).reshape(YBLK, NCOL // 2 * 256)
    ytab = np.stack(split_np(ytab))

    angle = turns(np.arange(NY, dtype=np.int64)[:, None] * YBLK, VSTEP * m[None, :], MOD)
    yrot = np.zeros((8, NCOL * SUB), np.float32)
    yrot[0:4] = np.cos(angle)
    yrot[4:8] = np.sin(angle)

    cells = np.arange(SUB, dtype=np.int64) - SUB // 2
    radius = cells[:, None] ** 2 + cells[None, :] ** 2
    theta = turns(np.arange(NW, dtype=np.int64)[:, None, None], radius[None], SUB * SUB)
    theta = theta.transpose(1, 0, 2).reshape(SUB, NW * SUB)
    screens = np.stack([np.cos(theta), np.sin(theta)]).astype(np.float32)

    index = np.arange(SUB, dtype=np.int64)
    angle = turns(index[:, None], index[None, :], SUB)
    dcos, dsin = np.cos(angle) / 16.0, np.sin(angle) / 16.0
    left = np.block([[dcos, dsin], [-dsin, dcos]]).astype(np.float32)
    zero = np.zeros_like(dcos)
    right = np.block([[dcos, zero, dsin, zero], [zero, dcos, zero, dsin]]).astype(np.float32)
    return xtab, xrot, ytab, yrot, screens, left, right


def row_order(x_lo, core):
    return [2 * (1 - x_lo) + 1 - core, 2 * x_lo + 1 - core, 2 * (1 - x_lo) + core, 2 * x_lo + core]


def split(values):
    high = values.astype(BF16)
    return high, (values - high.astype(F32)).astype(BF16)


def dot(a, b):
    return jnp.dot(a, b, preferred_element_type=F32)


def x_kernel(facet_ref, xtab_ref, xrot_ref, s0_ref, s1_ref, k0_ref, k1_ref, rot_ref):
    vis = lax.axis_index("vis")
    x_lo, core = vis // 2, vis % 2

    @pl.when(pl.program_id(0) == 0)
    def _():
        rot_ref[...] = xrot_ref[lax.axis_index("facet") * N_VIS + vis].T

    rhs = [split(facet_ref[0]), split(facet_ref[1])]
    order = row_order(x_lo, core)
    full = jnp.concatenate([xtab_ref[r] for r in order], 0)
    high = jnp.concatenate([xtab_ref[r, : 2 * SUB] for r in order], 0)
    a = []
    for hi, lo in rhs:
        both = dot(full, hi).reshape(N_VIS, 2, 2 * SUB, YBLK)
        a.append(both[:, 0] + both[:, 1] + dot(high, lo).reshape(N_VIS, 2 * SUB, YBLK))
    for i, out in enumerate((s0_ref, s1_ref, k0_ref, k1_ref)):
        re = a[0][i, :SUB] + a[1][i, SUB:]
        im = a[1][i, :SUB] - a[0][i, SUB:]
        cosine = rot_ref[i * SUB : (i + 1) * SUB, 0:1]
        sine = rot_ref[i * SUB : (i + 1) * SUB, 1:2]
        out[:SUB] = re * cosine + im * sine
        out[SUB:] = im * cosine - re * sine


def x_sum(facet_image, xtab, xrot):
    out = jax.ShapeDtypeStruct((2 * SUB, FP), F32)
    block = pl.BlockSpec((2 * SUB, YBLK), lambda i: (0, i))
    return pl.pallas_call(
        x_kernel,
        grid=(NY,),
        in_specs=[
            pl.BlockSpec((2, XROWS, YBLK), lambda i: (0, 0, i)),
            pl.BlockSpec(xtab.shape, lambda i: (0, 0, 0)),
            pl.BlockSpec(xrot.shape, lambda i: (0, 0, 0)),
        ],
        out_specs=[block] * 4,
        out_shape=[out] * 4,
        scratch_shapes=[pltpu.VMEM((N_VIS * SUB, 8), F32)],
        compiler_params=pltpu.CompilerParams(vmem_limit_bytes=VMEM_LIMIT),
        name="x_sum",
    )(facet_image, xtab, xrot)


def y_kernel(kept_ref, near_ref, far_ref, ytab_ref, yrot_ref, out_ref, lhs_ref):
    @pl.when(pl.program_id(0) == 0)
    def _():
        total = kept_ref[...] + near_ref[...] + far_ref[...]
        hi, lo = split(total)
        for y in range(NY):
            lhs_ref[y * 128 : (y + 1) * 128] = hi[:, y * YBLK : (y + 1) * YBLK]
            lhs_ref[NY * 128 + y * 128 : NY * 128 + (y + 1) * 128] = lo[:, y * YBLK : (y + 1) * YBLK]

    half = NY * 128
    both = dot(lhs_ref[...], ytab_ref[0])
    part = both[:half] + both[half:] + dot(lhs_ref[:half], ytab_ref[1])
    re = part[0:64, :128] + part[64:128, 128:]
    im = part[64:128, :128] - part[0:64, 128:]
    for y in range(1, NY):
        now = part[y * 128 : (y + 1) * 128]
        gre = now[0:64, :128] + now[64:128, 128:]
        gim = now[64:128, :128] - now[0:64, 128:]
        cosine = yrot_ref[y : y + 1]
        sine = yrot_ref[4 + y : 5 + y]
        re = re + gre * cosine + gim * sine
        im = im + gim * cosine - gre * sine
    first = lax.broadcasted_iota(jnp.int32, (64, 128), 1) < 64
    out_ref[0] = jnp.where(first, re, pltpu.roll(im, 64, 1))
    out_ref[1] = jnp.where(first, pltpu.roll(re, 64, 1), im)


def y_sum(kept, near, far, ytab, yrot):
    whole = pl.BlockSpec((2 * SUB, FP), lambda i: (0, 0))
    return pl.pallas_call(
        y_kernel,
        grid=(NCOL // 2,),
        in_specs=[
            whole,
            whole,
            whole,
            pl.BlockSpec((2, YBLK, 256), lambda i: (0, 0, i)),
            pl.BlockSpec((8, 128), lambda i: (0, i)),
        ],
        out_specs=pl.BlockSpec((2, SUB, 2 * SUB), lambda i: (i, 0, 0)),
        out_shape=jax.ShapeDtypeStruct((NCOL, SUB, 2 * SUB), F32),
        scratch_shapes=[pltpu.VMEM((2 * NY * 128, YBLK), BF16)],
        compiler_params=pltpu.CompilerParams(vmem_limit_bytes=VMEM_LIMIT),
        name="y_sum",
    )(kept, near, far, ytab, yrot)


TAPER = math.sqrt(0.5 * math.log2(math.e)) / 1.6


def degrid_kernel(
    lists_ref, counts_ref, wplanes_ref, owners_ref,
    blocks_ref, screens_ref, left_ref, right_ref, offsets_ref, frac_ref,
    out_ref, planes_ref, rows_ref, fill_ref,
):
    vis = lax.axis_index("vis")
    grid = blocks_ref[lists_ref[vis, 0]]
    for k in range(1, K):
        grid = grid + blocks_ref[lists_ref[vis, k]]
    turned = grid.T
    gre = jnp.concatenate([turned[:SUB]] * NW, 1)
    gim = jnp.concatenate([turned[SUB:]] * NW, 1)
    hre = gre * screens_ref[0] - gim * screens_ref[1]
    him = gre * screens_ref[1] + gim * screens_ref[0]
    along = jnp.dot(left_ref[...], jnp.concatenate([hre, him], 0), precision=HIGHEST, preferred_element_type=F32)
    first = lax.broadcasted_iota(jnp.int32, (128, 128), 1) < 64
    for pair in range(NW // 2):
        m = jnp.dot(along[:, pair * 128 : (pair + 1) * 128], right_ref[...], precision=HIGHEST, preferred_element_type=F32)
        re = m[:SUB, :128] + m[SUB:, 128:]
        im = m[SUB:, :128] - m[:SUB, 128:]
        both = jnp.concatenate([re, im], 0)
        swapped = pltpu.roll(both, 64, 1)
        for j, twice in enumerate((jnp.where(first, both, swapped), jnp.where(first, swapped, both))):
            hi, lo = split(twice)
            planes_ref[2 * pair + j, :, :128] = hi
            planes_ref[2 * pair + j, :, 128:] = lo

    rows_ref[...] = jnp.zeros_like(rows_ref)
    for o in range(N_VIS):
        fill_ref[o] = 0
    cell = lax.broadcasted_iota(jnp.int32, (8, CH), 0)
    count = counts_ref[0, 0]

    def taps(offset, frac):
        offset = jnp.broadcast_to(offset, (8, CH))
        shift = jnp.broadcast_to(frac, (8, CH))
        step = ((cell - offset) & 7).astype(F32)
        d = step * TAPER - shift
        value = jnp.exp2(-(d * d))
        return value, (offset - cell + 7) >> 3

    def body(group, carry):
        base = pl.multiple_of(group * 8, 8)
        ou = offsets_ref[0, 0, 0, pl.ds(base, 8), :]
        ov = offsets_ref[1, 0, 0, pl.ds(base, 8), :]
        fu = (frac_ref[0, 0, 0, pl.ds(base, 8), :] + 3.5) * TAPER
        fv = (frac_ref[1, 0, 0, pl.ds(base, 8), :] + 3.5) * TAPER
        for i in range(8):
            n = base + i
            uval, ublock = taps(ou[i : i + 1], fu[i : i + 1])
            vval, vblock = taps(ov[i : i + 1], fv[i : i + 1])
            uhi = uval.astype(BF16).astype(F32)
            ulo = uval - uhi
            zero = jnp.zeros_like(uhi)
            high = jnp.concatenate([jnp.where(ublock == j, uhi, zero) for j in range(8)], 0).astype(BF16)
            low = jnp.concatenate([jnp.where(ublock == j, ulo, zero) for j in range(8)], 0).astype(BF16)
            t = dot(planes_ref[wplanes_ref[0, 0, n], :, :192], jnp.concatenate([high, low, high], 0))
            are, aim = t[0:8], t[64:72]
            for j in range(1, 8):
                here = vblock == j
                are = jnp.where(here, t[8 * j : 8 * j + 8], are)
                aim = jnp.where(here, t[64 + 8 * j : 72 + 8 * j], aim)
            live = jnp.where(n < count, 1.0, 0.0)
            re = jnp.sum(are * vval, 0, keepdims=True) * live
            im = jnp.sum(aim * vval, 0, keepdims=True) * live
            owner = owners_ref[0, 0, n]
            slot = fill_ref[owner]
            fill_ref[owner] = slot + 1
            place = owner * (2 * CAP) + slot + (slot & ~7)
            rows_ref[pl.ds(place, 1), :] = re
            rows_ref[pl.ds(place + 8, 1), :] = im
        return carry

    lax.fori_loop(0, ROWS // 8, body, 0)

    tiles = rows_ref[...].reshape(N_VIS, CAP // 8, 2, 8, CH)
    out_ref[:, :, :CH] = tiles[:, :, 0].reshape(N_VIS, CAP, CH)
    out_ref[:, :, CH:] = tiles[:, :, 1].reshape(N_VIS, CAP, CH)


def degrid(lists, counts, wplanes, owners, blocks, screens, left, right, offsets, frac):
    smem = pl.BlockSpec(memory_space=pltpu.SMEM)
    vmem = pl.BlockSpec(memory_space=pltpu.VMEM)
    return pl.pallas_call(
        degrid_kernel,
        in_specs=[smem] * 4 + [vmem] * 6,
        out_specs=vmem,
        out_shape=jax.ShapeDtypeStruct((N_VIS, CAP, 2 * CH), F32),
        scratch_shapes=[pltpu.VMEM((NW, 128, 256), BF16), pltpu.VMEM((2 * N_VIS * CAP, CH), F32), pltpu.SMEM((N_VIS,), jnp.int32)],
        compiler_params=pltpu.CompilerParams(vmem_limit_bytes=VMEM_LIMIT),
        name="degrid",
    )(lists, counts, wplanes, owners, blocks, screens, left, right, offsets, frac)


TO_CORE = [(0, 1), (1, 0), (2, 3), (3, 2)]
TO_CHIP = [(0, 2), (2, 0), (1, 3), (3, 1)]


def on_device(facet_image, contributions, counts, wplanes, kernel_offsets, kernel_frac, owners):
    xtab, xrot, ytab, yrot, screens, left, right = [jnp.asarray(t) for t in tables()]
    s0, s1, k0, k1 = x_sum(facet_image, xtab, xrot)
    r0 = lax.ppermute(s0, "vis", TO_CORE)
    r1 = lax.ppermute(s1, "vis", TO_CORE)
    far = lax.ppermute(k0 + r0, "vis", TO_CHIP)
    blocks = y_sum(k1, r1, far, ytab, yrot)
    arrived = lax.all_to_all(blocks, "facet", split_axis=0, concat_axis=0, tiled=True)
    outgoing = degrid(
        contributions[:, 0, :], counts, wplanes, owners[..., 0], arrived, screens, left, right, kernel_offsets, kernel_frac
    )
    owned = lax.all_to_all(outgoing, "vis", split_axis=0, concat_axis=0, tiled=True)
    return owned.reshape(1, 1, N_VIS, CAP, 2 * CH)


def solution(mesh):
    return jax.shard_map(
        on_device,
        mesh=mesh,
        in_specs=(
            P(None, ("facet", "vis"), None),
            P(None, "facet", None),
            P("vis", "facet"),
            P("vis", "facet", None),
            P(None, "vis", "facet", None, None),
            P(None, "vis", "facet", None, None),
            P("vis", "facet", None, None),
        ),
        out_specs=P("vis", "facet", None, None, None),
        check_vma=False,
    )
```

```python
import functools
import math

import jax
import jax.numpy as jnp
import ml_dtypes
import numpy as np
from jax import lax
from jax.experimental import pallas as pl
from jax.experimental.pallas import tpu as pltpu
from jax.sharding import PartitionSpec as P

FP = 1024
SUB = 64
CH = 128
NW = 8
USTEP = 129
VSTEP = 33
ROWS = 512
K = 8
NCOL = 32
CAP = 256
N_FACET = 32
N_VIS = 4
MOD = FP * N_FACET
XROWS = FP // N_VIS
YBLK = 256
NY = FP // YBLK

F32 = jnp.float32
BF16 = jnp.bfloat16
HIGHEST = lax.Precision.HIGHEST
VMEM_LIMIT = 20 * 1024 * 1024


def turns(first, second, modulus):
    return 2.0 * math.pi * ((first * second) % modulus) / modulus


def split_np(values):
    high = values.astype(ml_dtypes.bfloat16)
    low = (values - high.astype(np.float64)).astype(ml_dtypes.bfloat16)
    return high, low


@functools.cache
def tables():
    freq = USTEP * np.arange(N_VIS * SUB, dtype=np.int64)
    theta = turns(freq[:, None], np.arange(XROWS, dtype=np.int64)[None, :], MOD).reshape(N_VIS, SUB, XROWS)
    ch, cl = split_np(np.cos(theta))
    sh, sl = split_np(np.sin(theta))
    xtab = np.concatenate([ch, sh, cl, sl], 1)

    xrot = np.zeros((N_FACET * N_VIS, 8, N_VIS * SUB), np.float32)
    for f in range(N_FACET):
        for v in range(N_VIS):
            order = row_order(v // 2, v % 2)
            rows = np.concatenate([freq[r * SUB : (r + 1) * SUB] for r in order])
            angle = turns(rows, f * FP + v * XROWS, MOD)
            xrot[f * N_VIS + v, 0] = np.cos(angle)
            xrot[f * N_VIS + v, 1] = np.sin(angle)

    m = np.arange(NCOL * SUB, dtype=np.int64)
    theta = turns(np.arange(YBLK, dtype=np.int64)[:, None], VSTEP * m[None, :], MOD).reshape(YBLK, NCOL // 2, 128)
    ytab = np.concatenate([np.cos(theta), np.sin(theta)], -1).transpose(1, 0, 2)
    ytab = np.stack(split_np(ytab), 1)

    angle = turns(np.arange(NY, dtype=np.int64)[:, None] * YBLK, VSTEP * m[None, :], MOD)
    yrot = np.zeros((8, NCOL * SUB), np.float32)
    yrot[0:4] = np.cos(angle)
    yrot[4:8] = np.sin(angle)

    cells = np.arange(SUB, dtype=np.int64) - SUB // 2
    radius = cells[:, None] ** 2 + cells[None, :] ** 2
    theta = turns(np.arange(NW, dtype=np.int64)[:, None, None], radius[None], SUB * SUB)
    theta = theta.transpose(1, 0, 2).reshape(SUB, NW * SUB)
    screens = np.stack([np.cos(theta), np.sin(theta)]).astype(np.float32)

    index = np.arange(SUB, dtype=np.int64)
    angle = turns(index[:, None], index[None, :], SUB)
    dcos, dsin = np.cos(angle) / 16.0, np.sin(angle) / 16.0
    left = np.block([[dcos, dsin], [-dsin, dcos]]).astype(np.float32)
    zero = np.zeros_like(dcos)
    right = np.block([[dcos, zero, dsin, zero], [zero, dcos, zero, dsin]]).astype(np.float32)
    return xtab, xrot, ytab, yrot, screens, left, right


def row_order(x_lo, core):
    return [2 * (1 - x_lo) + 1 - core, 2 * x_lo + 1 - core, 2 * (1 - x_lo) + core, 2 * x_lo + core]


def split(values):
    high = values.astype(BF16)
    return high, (values - high.astype(F32)).astype(BF16)


def dot(a, b):
    return jnp.dot(a, b, preferred_element_type=F32)


def x_kernel(facet_ref, xtab_ref, xrot_ref, s0_ref, s1_ref, k0_ref, k1_ref, rot_ref):
    vis = lax.axis_index("vis")
    x_lo, core = vis // 2, vis % 2

    @pl.when(pl.program_id(0) == 0)
    def _():
        rot_ref[...] = xrot_ref[lax.axis_index("facet") * N_VIS + vis].T

    rhs = [split(facet_ref[0]), split(facet_ref[1])]
    order = row_order(x_lo, core)
    full = jnp.concatenate([xtab_ref[r] for r in order], 0)
    high = jnp.concatenate([xtab_ref[r, : 2 * SUB] for r in order], 0)
    a = []
    for hi, lo in rhs:
        both = dot(full, hi).reshape(N_VIS, 2, 2 * SUB, YBLK)
        a.append(both[:, 0] + both[:, 1] + dot(high, lo).reshape(N_VIS, 2 * SUB, YBLK))
    for i, out in enumerate((s0_ref, s1_ref, k0_ref, k1_ref)):
        re = a[0][i, :SUB] + a[1][i, SUB:]
        im = a[1][i, :SUB] - a[0][i, SUB:]
        cosine = rot_ref[i * SUB : (i + 1) * SUB, 0:1]
        sine = rot_ref[i * SUB : (i + 1) * SUB, 1:2]
        out[:SUB] = re * cosine + im * sine
        out[SUB:] = im * cosine - re * sine


def x_sum(facet_image, xtab, xrot):
    out = jax.ShapeDtypeStruct((2 * SUB, FP), F32)
    block = pl.BlockSpec((2 * SUB, YBLK), lambda i: (0, i))
    return pl.pallas_call(
        x_kernel,
        grid=(NY,),
        in_specs=[
            pl.BlockSpec((2, XROWS, YBLK), lambda i: (0, 0, i)),
            pl.BlockSpec(xtab.shape, lambda i: (0, 0, 0)),
            pl.BlockSpec(xrot.shape, lambda i: (0, 0, 0)),
        ],
        out_specs=[block] * 4,
        out_shape=[out] * 4,
        scratch_shapes=[pltpu.VMEM((N_VIS * SUB, 8), F32)],
        compiler_params=pltpu.CompilerParams(vmem_limit_bytes=60 * 1024 * 1024),
        name="x_sum",
    )(facet_image, xtab, xrot)


def y_kernel(kept_ref, near_ref, far_ref, ytab_ref, yrot_ref, out_ref, lhs_ref):
    @pl.when(pl.program_id(0) == 0)
    def _():
        total = kept_ref[...] + near_ref[...] + far_ref[...]
        hi, lo = split(total)
        for y in range(NY):
            lhs_ref[y * 128 : (y + 1) * 128] = hi[:, y * YBLK : (y + 1) * YBLK]
            lhs_ref[NY * 128 + y * 128 : NY * 128 + (y + 1) * 128] = lo[:, y * YBLK : (y + 1) * YBLK]

    half = NY * 128
    first = lax.broadcasted_iota(jnp.int32, (64, 128), 1) < 64
    lhs = jnp.concatenate([lhs_ref[:half], lhs_ref[half:], lhs_ref[:half]], 1)
    for w in range(PAIRS):
        part = dot(lhs, jnp.concatenate([ytab_ref[w, 0], ytab_ref[w, 0], ytab_ref[w, 1]], 0))
        re = part[0:64, :128] + part[64:128, 128:]
        im = part[64:128, :128] - part[0:64, 128:]
        for y in range(1, NY):
            now = part[y * 128 : (y + 1) * 128]
            gre = now[0:64, :128] + now[64:128, 128:]
            gim = now[64:128, :128] - now[0:64, 128:]
            cosine = yrot_ref[y : y + 1, w * 128 : (w + 1) * 128]
            sine = yrot_ref[4 + y : 5 + y, w * 128 : (w + 1) * 128]
            re = re + gre * cosine + gim * sine
            im = im + gim * cosine - gre * sine
        out_ref[2 * w] = jnp.where(first, re, pltpu.roll(im, 64, 1))
        out_ref[2 * w + 1] = jnp.where(first, pltpu.roll(re, 64, 1), im)


PAIRS = 4


def y_sum(kept, near, far, ytab, yrot):
    whole = pl.BlockSpec((2 * SUB, FP), lambda i: (0, 0))
    return pl.pallas_call(
        y_kernel,
        grid=(NCOL // 2 // PAIRS,),
        in_specs=[
            whole,
            whole,
            whole,
            pl.BlockSpec((PAIRS, 2, YBLK, 256), lambda i: (i, 0, 0, 0)),
            pl.BlockSpec((8, 128 * PAIRS), lambda i: (0, i)),
        ],
        out_specs=pl.BlockSpec((2 * PAIRS, SUB, 2 * SUB), lambda i: (i, 0, 0)),
        out_shape=jax.ShapeDtypeStruct((NCOL, SUB, 2 * SUB), F32),
        scratch_shapes=[pltpu.VMEM((2 * NY * 128, YBLK), BF16)],
        compiler_params=pltpu.CompilerParams(vmem_limit_bytes=VMEM_LIMIT),
        name="y_sum",
    )(kept, near, far, ytab, yrot)


TAPER = math.sqrt(0.5 * math.log2(math.e)) / 1.6
STEP = 32
SPAN = ROWS + 2 * NW + 2 * STEP
JUNK = 2 * 2 * CAP


def order_kernel(counts_ref, wplanes_ref, owners_ref, row_ref, place_ref, ends_ref, key_ref, fill_ref):
    vis = lax.axis_index("vis")
    count = counts_ref[0, 0]
    for i in range(2 * NW):
        key_ref[i] = 0
    for i in range(N_VIS):
        fill_ref[i] = 0

    def clear(i, carry):
        for j in range(8):
            row_ref[i * 8 + j] = 0
            place_ref[i * 8 + j] = JUNK
        return carry

    lax.fori_loop(0, SPAN // 8, clear, 0)

    def tally(i, carry):
        for j in range(8):
            n = i * 8 + j
            key = wplanes_ref[0, 0, n] + NW * (1 - ((owners_ref[0, 0, n] ^ vis) >> 1))
            key_ref[key] = key_ref[key] + jnp.where(n < count, 1, 0)
        return carry

    lax.fori_loop(0, ROWS // 8, tally, 0)
    start = jnp.int32(0)
    for part in range(2):
        for w in range(NW):
            held = key_ref[part * NW + w]
            key_ref[part * NW + w] = start
            start = start + ((held + 1) & ~1)
        start = (start + STEP - 1) & ~(STEP - 1)
        ends_ref[part] = start // STEP

    def deal(i, carry):
        for j in range(8):
            n = i * 8 + j
            apart = owners_ref[0, 0, n] ^ vis
            slot = fill_ref[apart]
            fill_ref[apart] = slot + 1
            key = wplanes_ref[0, 0, n] + NW * (1 - (apart >> 1))
            at = jnp.where(n < count, key_ref[key], SPAN)
            key_ref[key] = key_ref[key] + jnp.where(n < count, 1, 0)
            row_ref[at] = n
            place_ref[at] = (apart & 1) * (2 * CAP) + slot + (slot & ~7)
        return carry

    lax.fori_loop(0, ROWS // 8, deal, 0)


def order_rows(counts, wplanes, owners):
    smem = pl.BlockSpec(memory_space=pltpu.SMEM)
    flat = jax.ShapeDtypeStruct((SPAN + 8,), jnp.int32)
    return pl.pallas_call(
        order_kernel,
        in_specs=[smem] * 3,
        out_specs=[smem] * 3,
        out_shape=[flat, flat, jax.ShapeDtypeStruct((2,), jnp.int32)],
        scratch_shapes=[pltpu.SMEM((2 * NW,), jnp.int32), pltpu.SMEM((N_VIS,), jnp.int32)],
        cost_estimate=pl.CostEstimate(flops=20_000_000, bytes_accessed=20_000_000, transcendentals=0),
        name="order_rows",
    )(counts, wplanes, owners)


def planes_kernel(lists_ref, blocks_ref, screens_ref, left_ref, right_ref, planes_ref):
    vis = lax.axis_index("vis")
    grid = blocks_ref[lists_ref[vis, 0]]
    for k in range(1, K):
        grid = grid + blocks_ref[lists_ref[vis, k]]
    turned = grid.T
    gre = jnp.concatenate([turned[:SUB]] * NW, 1)
    gim = jnp.concatenate([turned[SUB:]] * NW, 1)
    hre = gre * screens_ref[0] - gim * screens_ref[1]
    him = gre * screens_ref[1] + gim * screens_ref[0]
    along = jnp.dot(left_ref[...], jnp.concatenate([hre, him], 0), precision=HIGHEST, preferred_element_type=F32)
    first = lax.broadcasted_iota(jnp.int32, (128, 128), 1) < 64
    for pair in range(NW // 2):
        m = jnp.dot(along[:, pair * 128 : (pair + 1) * 128], right_ref[...], precision=HIGHEST, preferred_element_type=F32)
        re = m[:SUB, :128] + m[SUB:, 128:]
        im = m[SUB:, :128] - m[:SUB, 128:]
        both = jnp.concatenate([re, im], 0)
        swapped = pltpu.roll(both, 64, 1)
        for j, twice in enumerate((jnp.where(first, both, swapped), jnp.where(first, swapped, both))):
            hi, lo = split(twice)
            planes_ref[2 * pair + j, :, :128] = hi
            planes_ref[2 * pair + j, :, 128:] = lo


def make_planes(lists, blocks, screens, left, right):
    vmem = pl.BlockSpec(memory_space=pltpu.VMEM)
    return pl.pallas_call(
        planes_kernel,
        in_specs=[pl.BlockSpec(memory_space=pltpu.SMEM)] + [vmem] * 4,
        out_specs=vmem,
        out_shape=jax.ShapeDtypeStruct((NW, 128, 256), BF16),
        compiler_params=pltpu.CompilerParams(vmem_limit_bytes=VMEM_LIMIT),
        name="make_planes",
    )(lists, blocks, screens, left, right)


def degrid_kernel(
    row_ref, place_ref, ends_ref, wplanes_ref, planes_ref, offsets_ref, frac_ref, out0_ref, out1_ref, rows_ref, *, part
):
    rows_ref[...] = jnp.zeros_like(rows_ref)
    cell = lax.broadcasted_iota(jnp.int32, (8, CH), 0)
    ahead = cell - 7

    def taps(axis, n):
        offset = jnp.broadcast_to(offsets_ref[axis, 0, 0, pl.ds(n, 1), :], (8, CH))
        shift = (jnp.broadcast_to(frac_ref[axis, 0, 0, pl.ds(n, 1), :], (8, CH)) + 3.5) * TAPER
        step = ((cell - offset) & 7).astype(F32)
        d = step * TAPER - shift
        return jnp.exp2(-(d * d)), (offset - ahead) >> 3

    def body(group, carry):
        base = group * STEP
        for i in range(0, STEP, 2):
            pair = [row_ref[base + i], row_ref[base + i + 1]]
            sides, high, low = [], [], []
            for n in pair:
                uval, ublock = taps(0, n)
                uhi = uval.astype(BF16).astype(F32)
                ulo = uval - uhi
                zero = jnp.zeros_like(uhi)
                high.append(jnp.concatenate([jnp.where(ublock == j, uhi, zero) for j in range(8)], 0).astype(BF16))
                low.append(jnp.concatenate([jnp.where(ublock == j, ulo, zero) for j in range(8)], 0).astype(BF16))
            high = jnp.concatenate(high, 1)
            low = jnp.concatenate(low, 1)
            both = dot(planes_ref[wplanes_ref[0, 0, pair[0]], :, :192], jnp.concatenate([high, low, high], 0))
            for side, n in enumerate(pair):
                t = both[:, side * CH : (side + 1) * CH]
                vval, vblock = taps(1, n)
                are, aim = t[0:8], t[64:72]
                for j in range(1, 8):
                    here = vblock == j
                    are = jnp.where(here, t[8 * j : 8 * j + 8], are)
                    aim = jnp.where(here, t[64 + 8 * j : 72 + 8 * j], aim)
                place = place_ref[base + i + side]
                rows_ref[pl.ds(place, 1), :] = jnp.sum(are * vval, 0, keepdims=True)
                rows_ref[pl.ds(place + 8, 1), :] = jnp.sum(aim * vval, 0, keepdims=True)
        return carry

    lax.fori_loop(0 if part == 0 else ends_ref[0], ends_ref[part], body, 0)

    for side, out in enumerate((out0_ref, out1_ref)):
        tiles = rows_ref[side * 2 * CAP : (side + 1) * 2 * CAP].reshape(CAP // 8, 2, 8, CH)
        out[:, :CH] = tiles[:, 0].reshape(CAP, CH)
        out[:, CH:] = tiles[:, 1].reshape(CAP, CH)


def degrid(part, row, place, ends, wplanes, planes, offsets, frac):
    smem = pl.BlockSpec(memory_space=pltpu.SMEM)
    vmem = pl.BlockSpec(memory_space=pltpu.VMEM)
    out = jax.ShapeDtypeStruct((CAP, 2 * CH), F32)
    return pl.pallas_call(
        functools.partial(degrid_kernel, part=part),
        in_specs=[smem] * 4 + [vmem] * 3,
        out_specs=[vmem] * 2,
        out_shape=[out] * 2,
        scratch_shapes=[pltpu.VMEM((2 * 2 * CAP + 16, CH), F32)],
        compiler_params=pltpu.CompilerParams(vmem_limit_bytes=VMEM_LIMIT),
        cost_estimate=pl.CostEstimate(flops=4_000_000_000, bytes_accessed=2_000_000, transcendentals=0),
        name="degrid_" + ("far", "near")[part],
    )(row, place, ends, wplanes, planes, offsets, frac)


def gather_kernel(self_ref, core_ref, chip_ref, cross_ref, out_ref, sems):
    vis = lax.axis_index("vis")
    copies = [
        pltpu.make_async_copy(ref, out_ref.at[0, 0, vis ^ i], sems.at[i])
        for i, ref in enumerate((self_ref, core_ref, chip_ref, cross_ref))
    ]
    for copy in copies:
        copy.start()
    for copy in copies:
        copy.wait()


def gather_rows(*blocks):
    return pl.pallas_call(
        gather_kernel,
        in_specs=[pl.BlockSpec(memory_space=pltpu.VMEM)] * N_VIS,
        out_specs=pl.BlockSpec(memory_space=pl.ANY),
        out_shape=jax.ShapeDtypeStruct((1, 1, N_VIS, CAP, 2 * CH), F32),
        scratch_shapes=[pltpu.SemaphoreType.DMA((N_VIS,))],
        name="gather_rows",
    )(*blocks)


TO_CORE = [(0, 1), (1, 0), (2, 3), (3, 2)]
TO_CHIP = [(0, 2), (2, 0), (1, 3), (3, 1)]
TO_CROSS = [(0, 3), (3, 0), (1, 2), (2, 1)]


def on_device(facet_image, contributions, counts, wplanes, kernel_offsets, kernel_frac, owners):
    xtab, xrot, ytab, yrot, screens, left, right = [jnp.asarray(t) for t in tables()]
    s0, s1, k0, k1 = x_sum(facet_image, xtab, xrot)
    r0 = lax.ppermute(s0, "vis", TO_CORE)
    r1 = lax.ppermute(s1, "vis", TO_CORE)
    far = lax.ppermute(k0 + r0, "vis", TO_CHIP)
    blocks = y_sum(k1, r1, far, ytab, yrot)
    row, place, ends = order_rows(counts, wplanes, owners[..., 0])
    arrived = lax.all_to_all(blocks, "facet", split_axis=0, concat_axis=0, tiled=True)
    planes = make_planes(contributions[:, 0, :], arrived, screens, left, right)
    to_chip, to_cross = degrid(0, row, place, ends, wplanes, planes, kernel_offsets, kernel_frac)
    from_chip = lax.ppermute(to_chip, "vis", TO_CHIP)
    from_cross = lax.ppermute(to_cross, "vis", TO_CROSS)
    own, to_core = degrid(1, row, place, ends, wplanes, planes, kernel_offsets, kernel_frac)
    from_core = lax.ppermute(to_core, "vis", TO_CORE)
    return gather_rows(own, from_core, from_chip, from_cross)


def solution(mesh):
    return jax.shard_map(
        on_device,
        mesh=mesh,
        in_specs=(
            P(None, ("facet", "vis"), None),
            P(None, "facet", None),
            P("vis", "facet"),
            P("vis", "facet", None),
            P(None, "vis", "facet", None, None),
            P(None, "vis", "facet", None, None),
            P("vis", "facet", None, None),
        ),
        out_specs=P("vis", "facet", None, None, None),
        check_vma=False,
    )
```

```python
import functools
import math

import jax
import jax.numpy as jnp
import ml_dtypes
import numpy as np
from jax import lax
from jax.experimental import pallas as pl
from jax.experimental.pallas import tpu as pltpu
from jax.sharding import PartitionSpec as P

FP = 1024
SUB = 64
CH = 128
NW = 8
USTEP = 129
VSTEP = 33
ROWS = 512
K = 8
NCOL = 32
CAP = 256
N_FACET = 32
N_VIS = 4
MOD = FP * N_FACET
XROWS = FP // N_VIS
YBLK = 256
NY = FP // YBLK

F32 = jnp.float32
BF16 = jnp.bfloat16
HIGHEST = lax.Precision.HIGHEST
VMEM_LIMIT = 20 * 1024 * 1024


def turns(first, second, modulus):
    return 2.0 * math.pi * ((first * second) % modulus) / modulus


def split_np(values):
    high = values.astype(ml_dtypes.bfloat16)
    low = (values - high.astype(np.float64)).astype(ml_dtypes.bfloat16)
    return high, low


@functools.cache
def tables():
    freq = USTEP * np.arange(N_VIS * SUB, dtype=np.int64)
    theta = turns(freq[:, None], np.arange(XROWS, dtype=np.int64)[None, :], MOD).reshape(N_VIS, SUB, XROWS)
    ch, cl = split_np(np.cos(theta))
    sh, sl = split_np(np.sin(theta))
    xtab = np.concatenate([ch, sh, cl, sl], 1)

    xrot = np.zeros((N_FACET * N_VIS, 8, N_VIS * SUB), np.float32)
    for f in range(N_FACET):
        for v in range(N_VIS):
            order = row_order(v // 2, v % 2)
            rows = np.concatenate([freq[r * SUB : (r + 1) * SUB] for r in order])
            angle = turns(rows, f * FP + v * XROWS, MOD)
            xrot[f * N_VIS + v, 0] = np.cos(angle)
            xrot[f * N_VIS + v, 1] = np.sin(angle)

    m = np.arange(NCOL * SUB, dtype=np.int64)
    theta = turns(np.arange(YBLK, dtype=np.int64)[:, None], VSTEP * m[None, :], MOD).reshape(YBLK, NCOL // 2, 128)
    ytab = np.concatenate([np.cos(theta), np.sin(theta)], -1).transpose(1, 0, 2)
    ytab = np.stack(split_np(ytab), 1)

    angle = turns(np.arange(NY, dtype=np.int64)[:, None] * YBLK, VSTEP * m[None, :], MOD)
    yrot = np.zeros((8, NCOL * SUB), np.float32)
    yrot[0:4] = np.cos(angle)
    yrot[4:8] = np.sin(angle)

    cells = np.arange(SUB, dtype=np.int64) - SUB // 2
    radius = cells[:, None] ** 2 + cells[None, :] ** 2
    theta = turns(np.arange(NW, dtype=np.int64)[:, None, None], radius[None], SUB * SUB)
    theta = theta.transpose(1, 0, 2).reshape(SUB, NW * SUB)
    screens = np.stack([np.cos(theta), np.sin(theta)]).astype(np.float32)

    index = np.arange(SUB, dtype=np.int64)
    angle = turns(index[:, None], index[None, :], SUB)
    dcos, dsin = np.cos(angle) / 16.0, np.sin(angle) / 16.0
    left = np.block([[dcos, dsin], [-dsin, dcos]]).astype(np.float32)
    zero = np.zeros_like(dcos)
    right = np.block([[dcos, zero, dsin, zero], [zero, dcos, zero, dsin]]).astype(np.float32)
    return xtab, xrot, ytab, yrot, screens, left, right


def row_order(x_lo, core):
    return [2 * (1 - x_lo) + 1 - core, 2 * x_lo + 1 - core, 2 * (1 - x_lo) + core, 2 * x_lo + core]


def split(values):
    high = values.astype(BF16)
    return high, (values - high.astype(F32)).astype(BF16)


def dot(a, b):
    return jnp.dot(a, b, preferred_element_type=F32)


def x_kernel(facet_ref, xtab_ref, xrot_ref, send_ref, k0_ref, k1_ref, rhs_ref, tab_ref, turn_ref, rot_ref, sems, *, half):
    vis = lax.axis_index("vis")
    x_lo, core = vis // 2, vis % 2
    loads = [
        pltpu.make_async_copy(xtab_ref, tab_ref, sems.at[0]),
        pltpu.make_async_copy(xrot_ref.at[lax.axis_index("facet") * N_VIS + vis], turn_ref, sems.at[1]),
    ]
    for i in range(2):
        columns = pl.ds((2 * half + i) * YBLK, YBLK)
        loads.append(pltpu.make_async_copy(facet_ref.at[:, :, columns], rhs_ref.at[i], sems.at[2 + i]))
    for load in loads:
        load.start()
    loads[1].wait()
    rot_ref[...] = turn_ref[...].T
    loads[0].wait()
    order = row_order(x_lo, core)
    full = jnp.concatenate([tab_ref[r] for r in order], 0)
    high = jnp.concatenate([tab_ref[r, : 2 * SUB] for r in order], 0)
    outs = (send_ref.at[: 2 * SUB], send_ref.at[2 * SUB :], k0_ref, k1_ref)
    for block in range(2):
        loads[2 + block].wait()
        a = []
        for part in range(2):
            hi, lo = split(rhs_ref[block, part])
            both = dot(full, hi).reshape(N_VIS, 2, 2 * SUB, YBLK)
            a.append(both[:, 0] + both[:, 1] + dot(high, lo).reshape(N_VIS, 2 * SUB, YBLK))
        for i, out in enumerate(outs):
            re = a[0][i, :SUB] + a[1][i, SUB:]
            im = a[1][i, :SUB] - a[0][i, SUB:]
            cosine = rot_ref[i * SUB : (i + 1) * SUB, 0:1]
            sine = rot_ref[i * SUB : (i + 1) * SUB, 1:2]
            out[:SUB, block * YBLK : (block + 1) * YBLK] = re * cosine + im * sine
            out[SUB:, block * YBLK : (block + 1) * YBLK] = im * cosine - re * sine


def x_sum(half, facet_image, xtab, xrot):
    vmem = pl.BlockSpec(memory_space=pltpu.VMEM)
    kept = jax.ShapeDtypeStruct((2 * SUB, FP // 2), F32)
    return pl.pallas_call(
        functools.partial(x_kernel, half=half),
        in_specs=[pl.BlockSpec(memory_space=pltpu.HBM)] * 3,
        out_specs=[vmem] * 3,
        out_shape=[jax.ShapeDtypeStruct((4 * SUB, FP // 2), F32), kept, kept],
        scratch_shapes=[
            pltpu.VMEM((2, 2, XROWS, YBLK), F32),
            pltpu.VMEM(xtab.shape, BF16),
            pltpu.VMEM(xrot.shape[1:], F32),
            pltpu.VMEM((N_VIS * SUB, 8), F32),
            pltpu.SemaphoreType.DMA((4,)),
        ],
        compiler_params=pltpu.CompilerParams(vmem_limit_bytes=(60, 20)[half] * 1024 * 1024),
        cost_estimate=pl.CostEstimate(flops=2_000_000_000, bytes_accessed=2_000_000, transcendentals=0),
        name="x_sum_" + "ab"[half],
    )(facet_image, xtab, xrot)


PAIRS = 4


def y_kernel(*refs, half):
    if half == 0:
        kept_ref, near_ref, far_ref, ytab_ref, yrot_ref, out_ref, lhs_ref = refs
    else:
        kept_ref, near_ref, far_ref, ytab_ref, yrot_ref, first_ref, out_ref, lhs_ref = refs

    @pl.when(pl.program_id(0) == 0)
    def _():
        hi, lo = split(kept_ref[...] + near_ref[...] + far_ref[...])
        for y in range(2):
            now = slice(y * YBLK, (y + 1) * YBLK)
            lhs_ref[y * 128 : (y + 1) * 128] = jnp.concatenate([hi[:, now], lo[:, now], hi[:, now]], 1)

    left_half = lax.broadcasted_iota(jnp.int32, (64, 128), 1) < 64
    for w in range(PAIRS):
        part = dot(lhs_ref[...], jnp.concatenate([ytab_ref[w, 0], ytab_ref[w, 0], ytab_ref[w, 1]], 0))
        re = im = None
        for y in range(2):
            now = part[y * 128 : (y + 1) * 128]
            gre = now[0:64, :128] + now[64:128, 128:]
            gim = now[64:128, :128] - now[0:64, 128:]
            quarter = 2 * half + y
            if quarter == 0:
                re, im = gre, gim
                continue
            cosine = yrot_ref[quarter : quarter + 1, w * 128 : (w + 1) * 128]
            sine = yrot_ref[4 + quarter : 5 + quarter, w * 128 : (w + 1) * 128]
            turned_re, turned_im = gre * cosine + gim * sine, gim * cosine - gre * sine
            re, im = (turned_re, turned_im) if re is None else (re + turned_re, im + turned_im)
        even = jnp.where(left_half, re, pltpu.roll(im, 64, 1))
        odd = jnp.where(left_half, pltpu.roll(re, 64, 1), im)
        if half == 1:
            even, odd = even + first_ref[2 * w], odd + first_ref[2 * w + 1]
        out_ref[2 * w] = even
        out_ref[2 * w + 1] = odd


def y_sum(half, kept, received, far, ytab, yrot, *first):
    whole = pl.BlockSpec((2 * SUB, FP // 2), lambda i: (0, 0))
    columns = pl.BlockSpec((2 * PAIRS, SUB, 2 * SUB), lambda i: (i, 0, 0))
    return pl.pallas_call(
        functools.partial(y_kernel, half=half),
        grid=(NCOL // 2 // PAIRS,),
        in_specs=[
            whole,
            pl.BlockSpec((2 * SUB, FP // 2), lambda i: (1, 0)),
            whole,
            pl.BlockSpec((PAIRS, 2, YBLK, 256), lambda i: (i, 0, 0, 0)),
            pl.BlockSpec((8, 128 * PAIRS), lambda i: (0, i)),
        ]
        + [columns] * len(first),
        out_specs=columns,
        out_shape=jax.ShapeDtypeStruct((NCOL, SUB, 2 * SUB), F32),
        scratch_shapes=[pltpu.VMEM((2 * 128, 3 * YBLK), BF16)],
        compiler_params=pltpu.CompilerParams(vmem_limit_bytes=VMEM_LIMIT),
        cost_estimate=pl.CostEstimate(flops=3_000_000_000, bytes_accessed=6_000_000, transcendentals=0),
        name="y_sum_" + "ab"[half],
    )(kept, received, far, ytab, yrot, *first)


TAPER = math.sqrt(0.5 * math.log2(math.e)) / 1.6
STEP = 32
SPAN = ROWS + N_VIS * (NW + STEP)
ENDS = SPAN + 8
JUNK = 2 * CAP


def order_kernel(counts_ref, wplanes_ref, owners_ref, order_ref, key_ref, fill_ref):
    vis = lax.axis_index("vis")
    count = counts_ref[0, 0]
    for i in range(N_VIS * NW):
        key_ref[i] = 0
    for i in range(N_VIS):
        fill_ref[i] = 0

    def clear(i, carry):
        for j in range(8):
            order_ref[i * 8 + j] = JUNK * ROWS
        return carry

    lax.fori_loop(0, SPAN // 8, clear, 0)

    def tally(i, carry):
        for j in range(8):
            n = i * 8 + j
            key = wplanes_ref[0, 0, n] + NW * (3 - (owners_ref[0, 0, n] ^ vis))
            key_ref[key] = key_ref[key] + jnp.where(n < count, 1, 0)
        return carry

    lax.fori_loop(0, ROWS // 8, tally, 0)
    start = jnp.int32(0)
    order_ref[ENDS] = 0
    for part in range(N_VIS):
        for w in range(NW):
            held = key_ref[part * NW + w]
            key_ref[part * NW + w] = start
            start = start + ((held + 1) & ~1)
        start = (start + STEP - 1) & ~(STEP - 1)
        order_ref[ENDS + 1 + part] = start // STEP

    def deal(i, carry):
        for j in range(8):
            n = i * 8 + j
            apart = owners_ref[0, 0, n] ^ vis
            slot = fill_ref[apart]
            fill_ref[apart] = slot + 1
            key = wplanes_ref[0, 0, n] + NW * (3 - apart)
            at = jnp.where(n < count, key_ref[key], SPAN)
            key_ref[key] = key_ref[key] + jnp.where(n < count, 1, 0)
            order_ref[at] = (slot + (slot & ~7)) * ROWS + n
        return carry

    lax.fori_loop(0, ROWS // 8, deal, 0)


def order_rows(counts, wplanes, owners):
    smem = pl.BlockSpec(memory_space=pltpu.SMEM)
    return pl.pallas_call(
        order_kernel,
        in_specs=[smem] * 3,
        out_specs=smem,
        out_shape=jax.ShapeDtypeStruct((ENDS + 8,), jnp.int32),
        scratch_shapes=[pltpu.SMEM((N_VIS * NW,), jnp.int32), pltpu.SMEM((N_VIS,), jnp.int32)],
        cost_estimate=pl.CostEstimate(flops=20_000_000, bytes_accessed=20_000_000, transcendentals=0),
        compiler_params=pltpu.CompilerParams(vmem_limit_bytes=8 * 1024 * 1024),
        name="order_rows",
    )(counts, wplanes, owners)


def planes_kernel(lists_ref, blocks_ref, screens_ref, left_ref, right_ref, planes_ref):
    vis = lax.axis_index("vis")
    grid = blocks_ref[lists_ref[vis, 0]]
    for k in range(1, K):
        grid = grid + blocks_ref[lists_ref[vis, k]]
    turned = grid.T
    gre = jnp.concatenate([turned[:SUB]] * NW, 1)
    gim = jnp.concatenate([turned[SUB:]] * NW, 1)
    hre = gre * screens_ref[0] - gim * screens_ref[1]
    him = gre * screens_ref[1] + gim * screens_ref[0]
    along = jnp.dot(left_ref[...], jnp.concatenate([hre, him], 0), precision=HIGHEST, preferred_element_type=F32)
    first = lax.broadcasted_iota(jnp.int32, (128, 128), 1) < 64
    for pair in range(NW // 2):
        m = jnp.dot(along[:, pair * 128 : (pair + 1) * 128], right_ref[...], precision=HIGHEST, preferred_element_type=F32)
        re = m[:SUB, :128] + m[SUB:, 128:]
        im = m[SUB:, :128] - m[:SUB, 128:]
        both = jnp.concatenate([re, im], 0)
        swapped = pltpu.roll(both, 64, 1)
        for j, twice in enumerate((jnp.where(first, both, swapped), jnp.where(first, swapped, both))):
            hi, lo = split(twice)
            planes_ref[2 * pair + j, :, :128] = hi
            planes_ref[2 * pair + j, :, 128:] = lo


def make_planes(lists, blocks, screens, left, right):
    vmem = pl.BlockSpec(memory_space=pltpu.VMEM)
    return pl.pallas_call(
        planes_kernel,
        in_specs=[pl.BlockSpec(memory_space=pltpu.SMEM)] + [vmem] * 4,
        out_specs=vmem,
        out_shape=jax.ShapeDtypeStruct((NW, 128, 256), BF16),
        compiler_params=pltpu.CompilerParams(vmem_limit_bytes=VMEM_LIMIT),
        name="make_planes",
    )(lists, blocks, screens, left, right)


def degrid_kernel(
    order_ref, wplanes_ref, planes_ref, offsets_ref, frac_ref, out_ref, rows_ref, *, part
):
    rows_ref[...] = jnp.zeros_like(rows_ref)
    cell = lax.broadcasted_iota(jnp.int32, (8, CH), 0)
    ahead = cell - 7

    def taps(axis, n):
        offset = jnp.broadcast_to(offsets_ref[axis, 0, 0, pl.ds(n, 1), :], (8, CH))
        shift = (jnp.broadcast_to(frac_ref[axis, 0, 0, pl.ds(n, 1), :], (8, CH)) + 3.5) * TAPER
        step = ((cell - offset) & 7).astype(F32)
        d = step * TAPER - shift
        return jnp.exp2(-(d * d)), (offset - ahead) >> 3

    def body(group, carry):
        base = group * STEP
        for i in range(0, STEP, 2):
            packed = [order_ref[base + i], order_ref[base + i + 1]]
            pair = [word & (ROWS - 1) for word in packed]
            sides, high, low = [], [], []
            for n in pair:
                uval, ublock = taps(0, n)
                uhi = uval.astype(BF16).astype(F32)
                ulo = uval - uhi
                zero = jnp.zeros_like(uhi)
                high.append(jnp.concatenate([jnp.where(ublock == j, uhi, zero) for j in range(8)], 0).astype(BF16))
                low.append(jnp.concatenate([jnp.where(ublock == j, ulo, zero) for j in range(8)], 0).astype(BF16))
            high = jnp.concatenate(high, 1)
            low = jnp.concatenate(low, 1)
            both = dot(planes_ref[wplanes_ref[0, 0, pair[0]], :, :192], jnp.concatenate([high, low, high], 0))
            for side, n in enumerate(pair):
                t = both[:, side * CH : (side + 1) * CH]
                vval, vblock = taps(1, n)
                are, aim = t[0:8], t[64:72]
                for j in range(1, 8):
                    here = vblock == j
                    are = jnp.where(here, t[8 * j : 8 * j + 8], are)
                    aim = jnp.where(here, t[64 + 8 * j : 72 + 8 * j], aim)
                place = packed[side] >> 9
                rows_ref[pl.ds(place, 1), :] = jnp.sum(are * vval, 0, keepdims=True)
                rows_ref[pl.ds(place + 8, 1), :] = jnp.sum(aim * vval, 0, keepdims=True)
        return carry

    lax.fori_loop(order_ref[ENDS + part], order_ref[ENDS + part + 1], body, 0)

    tiles = rows_ref[: 2 * CAP].reshape(CAP // 8, 2, 8, CH)
    out_ref[:, :CH] = tiles[:, 0].reshape(CAP, CH)
    out_ref[:, CH:] = tiles[:, 1].reshape(CAP, CH)


def degrid(part, order, wplanes, planes, offsets, frac):
    smem = pl.BlockSpec(memory_space=pltpu.SMEM)
    vmem = pl.BlockSpec(memory_space=pltpu.VMEM)
    return pl.pallas_call(
        functools.partial(degrid_kernel, part=part),
        in_specs=[smem] * 2 + [vmem] * 3,
        out_specs=vmem,
        out_shape=jax.ShapeDtypeStruct((CAP, 2 * CH), F32),
        scratch_shapes=[pltpu.VMEM((2 * CAP + 16, CH), F32)],
        compiler_params=pltpu.CompilerParams(vmem_limit_bytes=VMEM_LIMIT),
        cost_estimate=pl.CostEstimate(flops=2_500_000_000, bytes_accessed=2_000_000, transcendentals=0),
        name="degrid_" + ("cross", "chip", "core", "own")[part],
    )(order, wplanes, planes, offsets, frac)


def gather_kernel(self_ref, core_ref, chip_ref, cross_ref, out_ref, sems):
    vis = lax.axis_index("vis")
    copies = [
        pltpu.make_async_copy(ref, out_ref.at[0, 0, vis ^ i], sems.at[i])
        for i, ref in enumerate((self_ref, core_ref, chip_ref, cross_ref))
    ]
    for copy in copies:
        copy.start()
    for copy in copies:
        copy.wait()


def gather_rows(*blocks):
    return pl.pallas_call(
        gather_kernel,
        in_specs=[pl.BlockSpec(memory_space=pltpu.VMEM)] * N_VIS,
        out_specs=pl.BlockSpec(memory_space=pl.ANY),
        out_shape=jax.ShapeDtypeStruct((1, 1, N_VIS, CAP, 2 * CH), F32),
        scratch_shapes=[pltpu.SemaphoreType.DMA((N_VIS,))],
        compiler_params=pltpu.CompilerParams(vmem_limit_bytes=8 * 1024 * 1024),
        name="gather_rows",
    )(*blocks)


TO_CORE = [(0, 1), (1, 0), (2, 3), (3, 2)]
TO_CHIP = [(0, 2), (2, 0), (1, 3), (3, 1)]
TO_CROSS = [(0, 3), (3, 0), (1, 2), (2, 1)]


def on_device(facet_image, contributions, counts, wplanes, kernel_offsets, kernel_frac, owners):
    xtab, xrot, ytab, yrot, screens, left, right = [jnp.asarray(t) for t in tables()]
    parts = []
    for half in range(2):
        send, k0, k1 = x_sum(half, facet_image, xtab, xrot)
        received = lax.ppermute(send, "vis", TO_CORE)
        far = lax.ppermute(k0 + received[: 2 * SUB], "vis", TO_CHIP)
        parts.append((k1, received, far))
    blocks = y_sum(0, *parts[0], ytab, yrot)
    blocks = y_sum(1, *parts[1], ytab, yrot, blocks)
    order = order_rows(counts, wplanes, owners[..., 0])
    arrived = lax.all_to_all(blocks, "facet", split_axis=0, concat_axis=0, tiled=True)
    planes = make_planes(contributions[:, 0, :], arrived, screens, left, right)
    to_cross, to_chip, to_core, own = [
        degrid(part, order, wplanes, planes, kernel_offsets, kernel_frac) for part in range(N_VIS)
    ]
    from_cross = lax.ppermute(to_cross, "vis", TO_CROSS)
    from_chip = lax.ppermute(to_chip, "vis", TO_CHIP)
    to_core, from_cross = lax.optimization_barrier((to_core, from_cross))
    from_core = lax.ppermute(to_core, "vis", TO_CORE)
    return gather_rows(own, from_core, from_chip, from_cross)


def solution(mesh):
    return jax.shard_map(
        on_device,
        mesh=mesh,
        in_specs=(
            P(None, ("facet", "vis"), None),
            P(None, "facet", None),
            P("vis", "facet"),
            P("vis", "facet", None),
            P(None, "vis", "facet", None, None),
            P(None, "vis", "facet", None, None),
            P("vis", "facet", None, None),
        ),
        out_specs=P("vis", "facet", None, None, None),
        check_vma=False,
    )
```

```python
import functools
import math

import jax
import jax.numpy as jnp
import ml_dtypes
import numpy as np
from jax import lax
from jax.experimental import pallas as pl
from jax.experimental.pallas import tpu as pltpu
from jax.sharding import PartitionSpec as P

FP = 1024
SUB = 64
CH = 128
NW = 8
USTEP = 129
VSTEP = 33
ROWS = 512
K = 8
NCOL = 32
CAP = 256
N_FACET = 32
N_VIS = 4
MOD = FP * N_FACET
XROWS = FP // N_VIS
YBLK = 256
NY = FP // YBLK

F32 = jnp.float32
BF16 = jnp.bfloat16
HIGHEST = lax.Precision.HIGHEST
VMEM_LIMIT = 20 * 1024 * 1024


def turns(first, second, modulus):
    return 2.0 * math.pi * ((first * second) % modulus) / modulus


def split_np(values):
    high = values.astype(ml_dtypes.bfloat16)
    low = (values - high.astype(np.float64)).astype(ml_dtypes.bfloat16)
    return high, low


@functools.cache
def tables():
    freq = USTEP * np.arange(N_VIS * SUB, dtype=np.int64)
    theta = turns(freq[:, None], np.arange(XROWS, dtype=np.int64)[None, :], MOD).reshape(N_VIS, SUB, XROWS)
    ch, cl = split_np(np.cos(theta))
    sh, sl = split_np(np.sin(theta))
    xtab = np.concatenate([ch, sh, cl, sl], 1)

    xrot = np.zeros((N_FACET * N_VIS, 8, N_VIS * SUB), np.float32)
    for f in range(N_FACET):
        for v in range(N_VIS):
            order = row_order(v // 2, v % 2)
            rows = np.concatenate([freq[r * SUB : (r + 1) * SUB] for r in order])
            angle = turns(rows, f * FP + v * XROWS, MOD)
            xrot[f * N_VIS + v, 0] = np.cos(angle)
            xrot[f * N_VIS + v, 1] = np.sin(angle)

    m = np.arange(NCOL * SUB, dtype=np.int64)
    theta = turns(np.arange(YBLK, dtype=np.int64)[:, None], VSTEP * m[None, :], MOD).reshape(YBLK, NCOL // 2, 128)
    ytab = np.concatenate([np.cos(theta), np.sin(theta)], -1).transpose(1, 0, 2)
    ytab = np.stack(split_np(ytab), 1)

    angle = turns(np.arange(NY, dtype=np.int64)[:, None] * YBLK, VSTEP * m[None, :], MOD)
    yrot = np.zeros((8, NCOL * SUB), np.float32)
    yrot[0:4] = np.cos(angle)
    yrot[4:8] = np.sin(angle)

    cells = np.arange(SUB, dtype=np.int64) - SUB // 2
    radius = cells[:, None] ** 2 + cells[None, :] ** 2
    theta = turns(np.arange(NW, dtype=np.int64)[:, None, None], radius[None], SUB * SUB)
    theta = theta.transpose(1, 0, 2).reshape(SUB, NW * SUB)
    screens = np.stack([np.cos(theta), np.sin(theta)]).astype(np.float32)

    index = np.arange(SUB, dtype=np.int64)
    angle = turns(index[:, None], index[None, :], SUB)
    dcos, dsin = np.cos(angle) / 16.0, np.sin(angle) / 16.0
    left = np.block([[dcos, dsin], [-dsin, dcos]]).astype(np.float32)
    zero = np.zeros_like(dcos)
    right = np.block([[dcos, zero, dsin, zero], [zero, dcos, zero, dsin]]).astype(np.float32)
    return xtab, xrot, ytab, yrot, screens, left, right


def row_order(x_lo, core):
    return [2 * (1 - x_lo) + 1 - core, 2 * x_lo + 1 - core, 2 * (1 - x_lo) + core, 2 * x_lo + core]


def split(values):
    high = values.astype(BF16)
    return high, (values - high.astype(F32)).astype(BF16)


def dot(a, b):
    return jnp.dot(a, b, preferred_element_type=F32)


def x_kernel(facet_ref, xtab_ref, xrot_ref, send_ref, k0_ref, k1_ref, rot_ref, *scratch, half):
    vis = lax.axis_index("vis")
    x_lo, core = vis // 2, vis % 2
    place = lax.axis_index("facet") * N_VIS + vis
    if half == 0:
        rhs_ref, tab_ref, turn_ref, sems = scratch
        loads = [
            pltpu.make_async_copy(xtab_ref, tab_ref, sems.at[0]),
            pltpu.make_async_copy(xrot_ref.at[place], turn_ref, sems.at[1]),
        ]
        for i in range(2):
            loads.append(
                pltpu.make_async_copy(facet_ref.at[i, :, pl.ds(0, FP // 2)], rhs_ref.at[i], sems.at[2 + i])
            )
        for load in loads:
            load.start()
        loads[1].wait()
        rot_ref[...] = turn_ref[...].T
        loads[0].wait()
    else:
        tab_ref = xtab_ref
        rot_ref[...] = xrot_ref[place].T
    order = row_order(x_lo, core)
    full = jnp.concatenate([tab_ref[r] for r in order], 0)
    high = jnp.concatenate([tab_ref[r, : 2 * SUB] for r in order], 0)
    outs = (send_ref.at[: 2 * SUB], send_ref.at[2 * SUB :], k0_ref, k1_ref)
    for block in range(2):
        if half == 0 and block == 0:
            loads[2].wait()
            loads[3].wait()
        a = []
        for part in range(2):
            if half == 0:
                values = rhs_ref[part, :, block * YBLK : (block + 1) * YBLK]
            else:
                values = facet_ref[part, :, (2 + block) * YBLK : (3 + block) * YBLK]
            hi, lo = split(values)
            both = dot(full, hi).reshape(N_VIS, 2, 2 * SUB, YBLK)
            a.append(both[:, 0] + both[:, 1] + dot(high, lo).reshape(N_VIS, 2 * SUB, YBLK))
        for i, out in enumerate(outs):
            re = a[0][i, :SUB] + a[1][i, SUB:]
            im = a[1][i, :SUB] - a[0][i, SUB:]
            cosine = rot_ref[i * SUB : (i + 1) * SUB, 0:1]
            sine = rot_ref[i * SUB : (i + 1) * SUB, 1:2]
            out[:SUB, block * YBLK : (block + 1) * YBLK] = re * cosine + im * sine
            out[SUB:, block * YBLK : (block + 1) * YBLK] = im * cosine - re * sine


def x_sum(half, facet_image, xtab, xrot):
    vmem = pl.BlockSpec(memory_space=pltpu.VMEM)
    kept = jax.ShapeDtypeStruct((2 * SUB, FP // 2), F32)
    copied = [
        pltpu.VMEM((2, XROWS, FP // 2), F32),
        pltpu.VMEM(xtab.shape, BF16),
        pltpu.VMEM(xrot.shape[1:], F32),
        pltpu.SemaphoreType.DMA((4,)),
    ]
    return pl.pallas_call(
        functools.partial(x_kernel, half=half),
        in_specs=[pl.BlockSpec(memory_space=pltpu.HBM) if half == 0 else vmem] * 3,
        out_specs=[vmem] * 3,
        out_shape=[jax.ShapeDtypeStruct((4 * SUB, FP // 2), F32), kept, kept],
        scratch_shapes=[pltpu.VMEM((N_VIS * SUB, 8), F32)] + (copied if half == 0 else []),
        compiler_params=pltpu.CompilerParams(vmem_limit_bytes=(60, 20)[half] * 1024 * 1024),
        cost_estimate=pl.CostEstimate(flops=2_000_000_000, bytes_accessed=2_000_000, transcendentals=0),
        name="x_sum_" + "ab"[half],
    )(facet_image, xtab, xrot)


def y_kernel(*refs, half):
    if half == 0:
        kept_ref, near_ref, far_ref, ytab_ref, yrot_ref, out_ref, lhs_ref = refs
    else:
        kept_ref, near_ref, far_ref, ytab_ref, yrot_ref, first_ref, out_ref, lhs_ref = refs

    hi, lo = split(kept_ref[...] + near_ref[2 * SUB :] + far_ref[...])
    lhs = []
    for y in range(2):
        now = slice(y * YBLK, (y + 1) * YBLK)
        lhs.append(jnp.concatenate([hi[:, now], lo[:, now], hi[:, now]], 1))
    lhs_ref[...] = jnp.concatenate(lhs, 0)

    left_half = lax.broadcasted_iota(jnp.int32, (64, 128), 1) < 64
    for w in range(NCOL // 2):
        part = dot(lhs_ref[...], jnp.concatenate([ytab_ref[w, 0], ytab_ref[w, 0], ytab_ref[w, 1]], 0))
        re = im = None
        for y in range(2):
            now = part[y * 128 : (y + 1) * 128]
            gre = now[0:64, :128] + now[64:128, 128:]
            gim = now[64:128, :128] - now[0:64, 128:]
            quarter = 2 * half + y
            if quarter == 0:
                re, im = gre, gim
                continue
            cosine = yrot_ref[quarter : quarter + 1, w * 128 : (w + 1) * 128]
            sine = yrot_ref[4 + quarter : 5 + quarter, w * 128 : (w + 1) * 128]
            turned_re, turned_im = gre * cosine + gim * sine, gim * cosine - gre * sine
            re, im = (turned_re, turned_im) if re is None else (re + turned_re, im + turned_im)
        even = jnp.where(left_half, re, pltpu.roll(im, 64, 1))
        odd = jnp.where(left_half, pltpu.roll(re, 64, 1), im)
        if half == 1:
            even, odd = even + first_ref[2 * w], odd + first_ref[2 * w + 1]
        out_ref[2 * w] = even
        out_ref[2 * w + 1] = odd


def y_sum(half, kept, received, far, ytab, yrot, *first):
    vmem = pl.BlockSpec(memory_space=pltpu.VMEM)
    return pl.pallas_call(
        functools.partial(y_kernel, half=half),
        in_specs=[vmem] * (5 + len(first)),
        out_specs=vmem,
        out_shape=jax.ShapeDtypeStruct((NCOL, SUB, 2 * SUB), F32),
        scratch_shapes=[pltpu.VMEM((2 * 128, 3 * YBLK), BF16)],
        compiler_params=pltpu.CompilerParams(vmem_limit_bytes=VMEM_LIMIT),
        cost_estimate=pl.CostEstimate(flops=3_000_000_000, bytes_accessed=6_000_000, transcendentals=0),
        name="y_sum_" + "ab"[half],
    )(kept, received, far, ytab, yrot, *first)


TAPER = math.sqrt(0.5 * math.log2(math.e)) / 1.6
STEP = 32
SPAN = ROWS + N_VIS * (NW + STEP)
ENDS = SPAN + 8
JUNK = 2 * CAP


def order_kernel(counts_ref, wplanes_ref, owners_ref, order_ref, key_ref, fill_ref):
    vis = lax.axis_index("vis")
    count = counts_ref[0, 0]
    for i in range(N_VIS * NW):
        key_ref[i] = 0
    for i in range(N_VIS):
        fill_ref[i] = 0

    def clear(i, carry):
        for j in range(8):
            order_ref[i * 8 + j] = JUNK * ROWS
        return carry

    lax.fori_loop(0, SPAN // 8, clear, 0)

    def tally(i, carry):
        for j in range(8):
            n = i * 8 + j
            key = wplanes_ref[0, 0, n] + NW * (3 - (owners_ref[0, 0, n] ^ vis))
            key_ref[key] = key_ref[key] + jnp.where(n < count, 1, 0)
        return carry

    lax.fori_loop(0, ROWS // 8, tally, 0)
    start = jnp.int32(0)
    order_ref[ENDS] = 0
    for part in range(N_VIS):
        for w in range(NW):
            held = key_ref[part * NW + w]
            key_ref[part * NW + w] = start
            start = start + ((held + 1) & ~1)
        start = (start + STEP - 1) & ~(STEP - 1)
        order_ref[ENDS + 1 + part] = start // STEP

    def deal(i, carry):
        for j in range(8):
            n = i * 8 + j
            apart = owners_ref[0, 0, n] ^ vis
            slot = fill_ref[apart]
            fill_ref[apart] = slot + 1
            key = wplanes_ref[0, 0, n] + NW * (3 - apart)
            at = jnp.where(n < count, key_ref[key], SPAN)
            key_ref[key] = key_ref[key] + jnp.where(n < count, 1, 0)
            order_ref[at] = (slot + (slot & ~7)) * ROWS + n
        return carry

    lax.fori_loop(0, ROWS // 8, deal, 0)


def order_rows(counts, wplanes, owners):
    smem = pl.BlockSpec(memory_space=pltpu.SMEM)
    return pl.pallas_call(
        order_kernel,
        in_specs=[smem] * 3,
        out_specs=smem,
        out_shape=jax.ShapeDtypeStruct((ENDS + 8,), jnp.int32),
        scratch_shapes=[pltpu.SMEM((N_VIS * NW,), jnp.int32), pltpu.SMEM((N_VIS,), jnp.int32)],
        cost_estimate=pl.CostEstimate(flops=20_000_000, bytes_accessed=20_000_000, transcendentals=0),
        compiler_params=pltpu.CompilerParams(vmem_limit_bytes=8 * 1024 * 1024),
        name="order_rows",
    )(counts, wplanes, owners)


def planes_kernel(lists_ref, blocks_ref, screens_ref, left_ref, right_ref, planes_ref):
    vis = lax.axis_index("vis")
    grid = blocks_ref[lists_ref[vis, 0]]
    for k in range(1, K):
        grid = grid + blocks_ref[lists_ref[vis, k]]
    turned = grid.T
    gre = jnp.concatenate([turned[:SUB]] * NW, 1)
    gim = jnp.concatenate([turned[SUB:]] * NW, 1)
    hre = gre * screens_ref[0] - gim * screens_ref[1]
    him = gre * screens_ref[1] + gim * screens_ref[0]
    along = jnp.dot(left_ref[...], jnp.concatenate([hre, him], 0), precision=HIGHEST, preferred_element_type=F32)
    first = lax.broadcasted_iota(jnp.int32, (128, 128), 1) < 64
    for pair in range(NW // 2):
        m = jnp.dot(along[:, pair * 128 : (pair + 1) * 128], right_ref[...], precision=HIGHEST, preferred_element_type=F32)
        re = m[:SUB, :128] + m[SUB:, 128:]
        im = m[SUB:, :128] - m[:SUB, 128:]
        both = jnp.concatenate([re, im], 0)
        swapped = pltpu.roll(both, 64, 1)
        for j, twice in enumerate((jnp.where(first, both, swapped), jnp.where(first, swapped, both))):
            hi, lo = split(twice)
            planes_ref[2 * pair + j, :, :128] = hi
            planes_ref[2 * pair + j, :, 128:] = lo


def make_planes(lists, blocks, screens, left, right):
    vmem = pl.BlockSpec(memory_space=pltpu.VMEM)
    return pl.pallas_call(
        planes_kernel,
        in_specs=[pl.BlockSpec(memory_space=pltpu.SMEM)] + [vmem] * 4,
        out_specs=vmem,
        out_shape=jax.ShapeDtypeStruct((NW, 128, 256), BF16),
        compiler_params=pltpu.CompilerParams(vmem_limit_bytes=VMEM_LIMIT),
        name="make_planes",
    )(lists, blocks, screens, left, right)


def degrid_kernel(
    order_ref, wplanes_ref, planes_ref, offsets_ref, frac_ref, out_ref, rows_ref, *, part
):
    rows_ref[...] = jnp.zeros_like(rows_ref)
    cell = lax.broadcasted_iota(jnp.int32, (8, CH), 0)
    ahead = cell - 7

    def taps(axis, n):
        offset = jnp.broadcast_to(offsets_ref[axis, 0, 0, pl.ds(n, 1), :], (8, CH))
        shift = (jnp.broadcast_to(frac_ref[axis, 0, 0, pl.ds(n, 1), :], (8, CH)) + 3.5) * TAPER
        step = ((cell - offset) & 7).astype(F32)
        d = step * TAPER - shift
        return jnp.exp2(-(d * d)), (offset - ahead) >> 3

    def body(group, carry):
        base = group * STEP
        for i in range(0, STEP, 2):
            packed = [order_ref[base + i], order_ref[base + i + 1]]
            pair = [word & (ROWS - 1) for word in packed]
            sides, high, low = [], [], []
            for n in pair:
                uval, ublock = taps(0, n)
                uhi = uval.astype(BF16).astype(F32)
                ulo = uval - uhi
                zero = jnp.zeros_like(uhi)
                high.append(jnp.concatenate([jnp.where(ublock == j, uhi, zero) for j in range(8)], 0).astype(BF16))
                low.append(jnp.concatenate([jnp.where(ublock == j, ulo, zero) for j in range(8)], 0).astype(BF16))
            high = jnp.concatenate(high, 1)
            low = jnp.concatenate(low, 1)
            both = dot(planes_ref[wplanes_ref[0, 0, pair[0]], :, :192], jnp.concatenate([high, low, high], 0))
            for side, n in enumerate(pair):
                t = both[:, side * CH : (side + 1) * CH]
                vval, vblock = taps(1, n)
                are, aim = t[0:8], t[64:72]
                for j in range(1, 8):
                    here = vblock == j
                    are = jnp.where(here, t[8 * j : 8 * j + 8], are)
                    aim = jnp.where(here, t[64 + 8 * j : 72 + 8 * j], aim)
                place = packed[side] >> 9
                rows_ref[pl.ds(place, 1), :] = jnp.sum(are * vval, 0, keepdims=True)
                rows_ref[pl.ds(place + 8, 1), :] = jnp.sum(aim * vval, 0, keepdims=True)
        return carry

    lax.fori_loop(order_ref[ENDS + part], order_ref[ENDS + part + 1], body, 0)

    tiles = rows_ref[: 2 * CAP].reshape(CAP // 8, 2, 8, CH)
    out_ref[:, :CH] = tiles[:, 0].reshape(CAP, CH)
    out_ref[:, CH:] = tiles[:, 1].reshape(CAP, CH)


def degrid(part, order, wplanes, planes, offsets, frac):
    smem = pl.BlockSpec(memory_space=pltpu.SMEM)
    vmem = pl.BlockSpec(memory_space=pltpu.VMEM)
    return pl.pallas_call(
        functools.partial(degrid_kernel, part=part),
        in_specs=[smem] * 2 + [vmem] * 3,
        out_specs=vmem,
        out_shape=jax.ShapeDtypeStruct((CAP, 2 * CH), F32),
        scratch_shapes=[pltpu.VMEM((2 * CAP + 16, CH), F32)],
        compiler_params=pltpu.CompilerParams(vmem_limit_bytes=VMEM_LIMIT),
        cost_estimate=pl.CostEstimate(flops=2_500_000_000, bytes_accessed=2_000_000, transcendentals=0),
        name="degrid_" + ("cross", "chip", "core", "own")[part],
    )(order, wplanes, planes, offsets, frac)


def gather_kernel(self_ref, core_ref, chip_ref, cross_ref, out_ref, sems):
    vis = lax.axis_index("vis")
    copies = [
        pltpu.make_async_copy(ref, out_ref.at[0, 0, vis ^ i], sems.at[i])
        for i, ref in enumerate((self_ref, core_ref, chip_ref, cross_ref))
    ]
    for copy in copies:
        copy.start()
    for copy in copies:
        copy.wait()


def gather_rows(*blocks):
    return pl.pallas_call(
        gather_kernel,
        in_specs=[pl.BlockSpec(memory_space=pltpu.VMEM)] * N_VIS,
        out_specs=pl.BlockSpec(memory_space=pl.ANY),
        out_shape=jax.ShapeDtypeStruct((1, 1, N_VIS, CAP, 2 * CH), F32),
        scratch_shapes=[pltpu.SemaphoreType.DMA((N_VIS,))],
        compiler_params=pltpu.CompilerParams(vmem_limit_bytes=8 * 1024 * 1024),
        name="gather_rows",
    )(*blocks)


TO_CORE = [(0, 1), (1, 0), (2, 3), (3, 2)]
TO_CHIP = [(0, 2), (2, 0), (1, 3), (3, 1)]
TO_CROSS = [(0, 3), (3, 0), (1, 2), (2, 1)]


def on_device(facet_image, contributions, counts, wplanes, kernel_offsets, kernel_frac, owners):
    xtab, xrot, ytab, yrot, screens, left, right = [jnp.asarray(t) for t in tables()]
    parts = []
    for half in range(2):
        send, k0, k1 = x_sum(half, facet_image, xtab, xrot)
        received = lax.ppermute(send, "vis", TO_CORE)
        far = lax.ppermute(k0 + received[: 2 * SUB], "vis", TO_CHIP)
        parts.append((k1, received, far))
    blocks = y_sum(0, *parts[0], ytab, yrot)
    blocks = y_sum(1, *parts[1], ytab, yrot, blocks)
    order = order_rows(counts, wplanes, owners[..., 0])
    arrived = lax.all_to_all(blocks, "facet", split_axis=0, concat_axis=0, tiled=True)
    planes = make_planes(contributions[:, 0, :], arrived, screens, left, right)
    to_cross, to_chip, to_core, own = [
        degrid(part, order, wplanes, planes, kernel_offsets, kernel_frac) for part in range(N_VIS)
    ]
    from_cross = lax.ppermute(to_cross, "vis", TO_CROSS)
    from_chip = lax.ppermute(to_chip, "vis", TO_CHIP)
    to_core, from_cross = lax.optimization_barrier((to_core, from_cross))
    from_core = lax.ppermute(to_core, "vis", TO_CORE)
    return gather_rows(own, from_core, from_chip, from_cross)


def solution(mesh):
    return jax.shard_map(
        on_device,
        mesh=mesh,
        in_specs=(
            P(None, ("facet", "vis"), None),
            P(None, "facet", None),
            P("vis", "facet"),
            P("vis", "facet", None),
            P(None, "vis", "facet", None, None),
            P(None, "vis", "facet", None, None),
            P("vis", "facet", None, None),
        ),
        out_specs=P("vis", "facet", None, None, None),
        check_vma=False,
    )
```

```python
import functools
import math

import jax
import jax.numpy as jnp
import ml_dtypes
import numpy as np
from jax import lax
from jax.experimental import pallas as pl
from jax.experimental.pallas import tpu as pltpu
from jax.sharding import PartitionSpec as P

FP = 1024
SUB = 64
CH = 128
NW = 8
USTEP = 129
VSTEP = 33
ROWS = 512
K = 8
NCOL = 32
CAP = 256
N_FACET = 32
N_VIS = 4
MOD = FP * N_FACET
XROWS = FP // N_VIS
YBLK = 256
NY = FP // YBLK

F32 = jnp.float32
BF16 = jnp.bfloat16
HIGHEST = lax.Precision.HIGHEST
VMEM_LIMIT = 20 * 1024 * 1024


def turns(first, second, modulus):
    return 2.0 * math.pi * ((first * second) % modulus) / modulus


def split_np(values):
    high = values.astype(ml_dtypes.bfloat16)
    low = (values - high.astype(np.float64)).astype(ml_dtypes.bfloat16)
    return high, low


@functools.cache
def tables():
    freq = USTEP * np.arange(N_VIS * SUB, dtype=np.int64)
    theta = turns(freq[:, None], np.arange(XROWS, dtype=np.int64)[None, :], MOD).reshape(N_VIS, SUB, XROWS)
    ch, cl = split_np(np.cos(theta))
    sh, sl = split_np(np.sin(theta))
    xtab = np.concatenate([ch, sh, cl, sl], 1)

    xrot = np.zeros((N_FACET * N_VIS, 8, N_VIS * SUB), np.float32)
    for f in range(N_FACET):
        for v in range(N_VIS):
            order = row_order(v // 2, v % 2)
            rows = np.concatenate([freq[r * SUB : (r + 1) * SUB] for r in order])
            angle = turns(rows, f * FP + v * XROWS, MOD)
            xrot[f * N_VIS + v, 0] = np.cos(angle)
            xrot[f * N_VIS + v, 1] = np.sin(angle)

    m = np.arange(NCOL * SUB, dtype=np.int64)
    theta = turns(np.arange(YBLK, dtype=np.int64)[:, None], VSTEP * m[None, :], MOD).reshape(YBLK, NCOL // 2, 128)
    ytab = np.concatenate([np.cos(theta), np.sin(theta)], -1).transpose(1, 0, 2)
    ytab = np.stack(split_np(ytab), 1)

    angle = turns(np.arange(NY, dtype=np.int64)[:, None] * YBLK, VSTEP * m[None, :], MOD)
    yrot = np.zeros((8, NCOL * SUB), np.float32)
    yrot[0:4] = np.cos(angle)
    yrot[4:8] = np.sin(angle)

    cells = np.arange(SUB, dtype=np.int64) - SUB // 2
    radius = cells[:, None] ** 2 + cells[None, :] ** 2
    theta = turns(np.arange(NW, dtype=np.int64)[:, None, None], radius[None], SUB * SUB)
    theta = theta.transpose(1, 0, 2).reshape(SUB, NW * SUB)
    screens = np.stack([np.cos(theta), np.sin(theta)]).astype(np.float32)

    index = np.arange(SUB, dtype=np.int64)
    angle = turns(index[:, None], index[None, :], SUB)
    dcos, dsin = np.cos(angle) / 16.0, np.sin(angle) / 16.0
    left = np.block([[dcos, dsin], [-dsin, dcos]]).astype(np.float32)
    zero = np.zeros_like(dcos)
    right = np.block([[dcos, zero, dsin, zero], [zero, dcos, zero, dsin]]).astype(np.float32)
    return xtab, xrot, ytab, yrot, screens, left, right


def row_order(x_lo, core):
    return [2 * (1 - x_lo) + 1 - core, 2 * x_lo + 1 - core, 2 * (1 - x_lo) + core, 2 * x_lo + core]


def split(values):
    high = values.astype(BF16)
    return high, (values - high.astype(F32)).astype(BF16)


def dot(a, b):
    return jnp.dot(a, b, preferred_element_type=F32)


def dot3(a, b):
    a_hi, a_lo = split(a)
    b_hi, b_lo = split(b)
    return dot(jnp.concatenate([a_hi, a_lo, a_hi], 1), jnp.concatenate([b_hi, b_hi, b_lo], 0))


def x_kernel(facet_ref, xtab_ref, xrot_ref, send_ref, k0_ref, k1_ref, rot_ref, *scratch, half):
    vis = lax.axis_index("vis")
    x_lo, core = vis // 2, vis % 2
    place = lax.axis_index("facet") * N_VIS + vis
    if half == 0:
        rhs_ref, tab_ref, turn_ref, sems = scratch
        loads = [
            pltpu.make_async_copy(xtab_ref, tab_ref, sems.at[0]),
            pltpu.make_async_copy(xrot_ref.at[place], turn_ref, sems.at[1]),
        ]
        for i in range(2):
            loads.append(
                pltpu.make_async_copy(facet_ref.at[i, :, pl.ds(0, FP // 2)], rhs_ref.at[i], sems.at[2 + i])
            )
        for load in loads:
            load.start()
        loads[1].wait()
        rot_ref[...] = turn_ref[...].T
        loads[0].wait()
    else:
        tab_ref = xtab_ref
        rot_ref[...] = xrot_ref[place].T
    order = row_order(x_lo, core)
    full = jnp.concatenate([tab_ref[r] for r in order], 0)
    high = jnp.concatenate([tab_ref[r, : 2 * SUB] for r in order], 0)
    outs = (send_ref.at[: 2 * SUB], send_ref.at[2 * SUB :], k0_ref, k1_ref)
    for block in range(2):
        if half == 0 and block == 0:
            loads[2].wait()
            loads[3].wait()
        a = []
        for part in range(2):
            if half == 0:
                values = rhs_ref[part, :, block * YBLK : (block + 1) * YBLK]
            else:
                values = facet_ref[part, :, (2 + block) * YBLK : (3 + block) * YBLK]
            hi, lo = split(values)
            both = dot(full, hi).reshape(N_VIS, 2, 2 * SUB, YBLK)
            a.append(both[:, 0] + both[:, 1] + dot(high, lo).reshape(N_VIS, 2 * SUB, YBLK))
        for i, out in enumerate(outs):
            re = a[0][i, :SUB] + a[1][i, SUB:]
            im = a[1][i, :SUB] - a[0][i, SUB:]
            cosine = rot_ref[i * SUB : (i + 1) * SUB, 0:1]
            sine = rot_ref[i * SUB : (i + 1) * SUB, 1:2]
            out[:SUB, block * YBLK : (block + 1) * YBLK] = re * cosine + im * sine
            out[SUB:, block * YBLK : (block + 1) * YBLK] = im * cosine - re * sine


def x_sum(half, facet_image, xtab, xrot):
    vmem = pl.BlockSpec(memory_space=pltpu.VMEM)
    kept = jax.ShapeDtypeStruct((2 * SUB, FP // 2), F32)
    copied = [
        pltpu.VMEM((2, XROWS, FP // 2), F32),
        pltpu.VMEM(xtab.shape, BF16),
        pltpu.VMEM(xrot.shape[1:], F32),
        pltpu.SemaphoreType.DMA((4,)),
    ]
    return pl.pallas_call(
        functools.partial(x_kernel, half=half),
        in_specs=[pl.BlockSpec(memory_space=pltpu.HBM) if half == 0 else vmem] * 3,
        out_specs=[vmem] * 3,
        out_shape=[jax.ShapeDtypeStruct((4 * SUB, FP // 2), F32), kept, kept],
        scratch_shapes=[pltpu.VMEM((N_VIS * SUB, 8), F32)] + (copied if half == 0 else []),
        compiler_params=pltpu.CompilerParams(vmem_limit_bytes=(60, 20)[half] * 1024 * 1024),
        cost_estimate=pl.CostEstimate(flops=2_000_000_000, bytes_accessed=2_000_000, transcendentals=0),
        name="x_sum_" + "ab"[half],
    )(facet_image, xtab, xrot)


def y_kernel(*refs, half):
    if half == 0:
        kept_ref, near_ref, far_ref, ytab_ref, yrot_ref, out_ref, lhs_ref = refs
    else:
        kept_ref, near_ref, far_ref, ytab_ref, yrot_ref, first_ref, sent_ref, lhs_ref, out_ref, sems = refs
    copies = []

    hi, lo = split(kept_ref[...] + near_ref[2 * SUB :] + far_ref[...])
    lhs = []
    for y in range(2):
        now = slice(y * YBLK, (y + 1) * YBLK)
        lhs.append(jnp.concatenate([hi[:, now], lo[:, now], hi[:, now]], 1))
    lhs_ref[...] = jnp.concatenate(lhs, 0)

    left_half = lax.broadcasted_iota(jnp.int32, (64, 128), 1) < 64
    for w in range(NCOL // 2):
        part = dot(lhs_ref[...], jnp.concatenate([ytab_ref[w, 0], ytab_ref[w, 0], ytab_ref[w, 1]], 0))
        re = im = None
        for y in range(2):
            now = part[y * 128 : (y + 1) * 128]
            gre = now[0:64, :128] + now[64:128, 128:]
            gim = now[64:128, :128] - now[0:64, 128:]
            quarter = 2 * half + y
            if quarter == 0:
                re, im = gre, gim
                continue
            cosine = yrot_ref[quarter : quarter + 1, w * 128 : (w + 1) * 128]
            sine = yrot_ref[4 + quarter : 5 + quarter, w * 128 : (w + 1) * 128]
            turned_re, turned_im = gre * cosine + gim * sine, gim * cosine - gre * sine
            re, im = (turned_re, turned_im) if re is None else (re + turned_re, im + turned_im)
        even = jnp.where(left_half, re, pltpu.roll(im, 64, 1))
        odd = jnp.where(left_half, pltpu.roll(re, 64, 1), im)
        if half == 1:
            even, odd = even + first_ref[2 * w], odd + first_ref[2 * w + 1]
        out_ref[2 * w] = even
        out_ref[2 * w + 1] = odd
        if half == 1 and w % 4 == 3:
            columns = pl.ds(2 * w - 6, 8)
            copies.append(pltpu.make_async_copy(out_ref.at[columns], sent_ref.at[columns], sems.at[w // 4]))
            copies[-1].start()
    for copy in copies:
        copy.wait()


def y_sum(half, kept, received, far, ytab, yrot, *first):
    vmem = pl.BlockSpec(memory_space=pltpu.VMEM)
    sending = [pltpu.VMEM((NCOL, SUB, 2 * SUB), F32), pltpu.SemaphoreType.DMA((NCOL // 8,))]
    return pl.pallas_call(
        functools.partial(y_kernel, half=half),
        in_specs=[vmem] * (5 + len(first)),
        out_specs=vmem if half == 0 else pl.BlockSpec(memory_space=pl.ANY),
        out_shape=jax.ShapeDtypeStruct((NCOL, SUB, 2 * SUB), F32),
        scratch_shapes=[pltpu.VMEM((2 * 128, 3 * YBLK), BF16)] + (sending if half == 1 else []),
        compiler_params=pltpu.CompilerParams(vmem_limit_bytes=VMEM_LIMIT),
        cost_estimate=pl.CostEstimate(flops=3_000_000_000, bytes_accessed=6_000_000, transcendentals=0),
        name="y_sum_" + "ab"[half],
    )(kept, received, far, ytab, yrot, *first)


TAPER = -0.5 * math.log2(math.e) / 1.6**2
STEP = 32
SPAN = ROWS + N_VIS * (NW + STEP)
ENDS = SPAN + 8
JUNK = 2 * CAP


def order_kernel(counts_ref, wplanes_ref, owners_ref, order_ref, key_ref, fill_ref):
    vis = lax.axis_index("vis")
    count = counts_ref[0, 0]
    for i in range(N_VIS * NW):
        key_ref[i] = 0
    for i in range(N_VIS):
        fill_ref[i] = 0

    def clear(i, carry):
        for j in range(8):
            order_ref[i * 8 + j] = JUNK * ROWS
        return carry

    lax.fori_loop(0, SPAN // 8, clear, 0)

    def tally(i, carry):
        for j in range(8):
            n = i * 8 + j
            key = wplanes_ref[0, 0, n] + NW * (3 - (owners_ref[0, 0, n] ^ vis))
            key_ref[key] = key_ref[key] + jnp.where(n < count, 1, 0)
        return carry

    lax.fori_loop(0, ROWS // 8, tally, 0)
    start = jnp.int32(0)
    order_ref[ENDS] = 0
    for part in range(N_VIS):
        for w in range(NW):
            held = key_ref[part * NW + w]
            key_ref[part * NW + w] = start
            start = start + ((held + 1) & ~1)
        start = (start + STEP - 1) & ~(STEP - 1)
        order_ref[ENDS + 1 + part] = start // STEP

    def deal(i, carry):
        for j in range(8):
            n = i * 8 + j
            apart = owners_ref[0, 0, n] ^ vis
            slot = fill_ref[apart]
            fill_ref[apart] = slot + 1
            key = wplanes_ref[0, 0, n] + NW * (3 - apart)
            at = jnp.where(n < count, key_ref[key], SPAN)
            key_ref[key] = key_ref[key] + jnp.where(n < count, 1, 0)
            order_ref[at] = (slot + (slot & ~7)) * ROWS + n
        return carry

    lax.fori_loop(0, ROWS // 8, deal, 0)


def order_rows(counts, wplanes, owners):
    smem = pl.BlockSpec(memory_space=pltpu.SMEM)
    return pl.pallas_call(
        order_kernel,
        in_specs=[smem] * 3,
        out_specs=smem,
        out_shape=jax.ShapeDtypeStruct((ENDS + 8,), jnp.int32),
        scratch_shapes=[pltpu.SMEM((N_VIS * NW,), jnp.int32), pltpu.SMEM((N_VIS,), jnp.int32)],
        cost_estimate=pl.CostEstimate(flops=20_000_000, bytes_accessed=20_000_000, transcendentals=0),
        compiler_params=pltpu.CompilerParams(vmem_limit_bytes=8 * 1024 * 1024),
        name="order_rows",
    )(counts, wplanes, owners)


def planes_kernel(lists_ref, blocks_ref, screens_ref, left_ref, right_ref, planes_ref):
    vis = lax.axis_index("vis")
    grid = blocks_ref[lists_ref[vis, 0]]
    for k in range(1, K):
        grid = grid + blocks_ref[lists_ref[vis, k]]
    turned = grid.T
    gre = jnp.concatenate([turned[:SUB]] * NW, 1)
    gim = jnp.concatenate([turned[SUB:]] * NW, 1)
    hre = gre * screens_ref[0] - gim * screens_ref[1]
    him = gre * screens_ref[1] + gim * screens_ref[0]
    along = dot3(left_ref[...], jnp.concatenate([hre, him], 0))
    first = lax.broadcasted_iota(jnp.int32, (128, 128), 1) < 64
    for pair in range(NW // 2):
        m = dot3(along[:, pair * 128 : (pair + 1) * 128], right_ref[...])
        re = m[:SUB, :128] + m[SUB:, 128:]
        im = m[SUB:, :128] - m[:SUB, 128:]
        both = jnp.concatenate([re, im], 0)
        swapped = pltpu.roll(both, 64, 1)
        for j, twice in enumerate((jnp.where(first, both, swapped), jnp.where(first, swapped, both))):
            hi, lo = split(twice)
            planes_ref[2 * pair + j, :, :128] = hi
            planes_ref[2 * pair + j, :, 128:] = lo


def make_planes(lists, blocks, screens, left, right):
    vmem = pl.BlockSpec(memory_space=pltpu.VMEM)
    return pl.pallas_call(
        planes_kernel,
        in_specs=[pl.BlockSpec(memory_space=pltpu.SMEM)] + [vmem] * 4,
        out_specs=vmem,
        out_shape=jax.ShapeDtypeStruct((NW, 128, 256), BF16),
        compiler_params=pltpu.CompilerParams(vmem_limit_bytes=VMEM_LIMIT),
        name="make_planes",
    )(lists, blocks, screens, left, right)


def degrid_kernel(
    order_ref, wplanes_ref, planes_ref, offsets_ref, frac_ref, out_ref, rows_ref, *, part
):
    rows_ref[...] = jnp.zeros_like(rows_ref)
    cell = lax.broadcasted_iota(jnp.int32, (8, CH), 0)
    ahead = cell - 7

    def taps(axis, n):
        offset = jnp.broadcast_to(offsets_ref[axis, 0, 0, pl.ds(n, 1), :], (8, CH))
        shift = jnp.broadcast_to(frac_ref[axis, 0, 0, pl.ds(n, 1), :], (8, CH)) + 3.5
        d = ((cell - offset) & 7).astype(F32) - shift
        return jnp.exp2(d * d * TAPER), (offset - ahead) >> 3

    def body(group, carry):
        base = group * STEP
        for i in range(0, STEP, 2):
            packed = [order_ref[base + i], order_ref[base + i + 1]]
            pair = [word & (ROWS - 1) for word in packed]
            sides, high, low = [], [], []
            for n in pair:
                uval, ublock = taps(0, n)
                uhi = uval.astype(BF16).astype(F32)
                ulo = uval - uhi
                zero = jnp.zeros_like(uhi)
                high.append(jnp.concatenate([jnp.where(ublock == j, uhi, zero) for j in range(8)], 0).astype(BF16))
                low.append(jnp.concatenate([jnp.where(ublock == j, ulo, zero) for j in range(8)], 0).astype(BF16))
            high = jnp.concatenate(high, 1)
            low = jnp.concatenate(low, 1)
            both = dot(planes_ref[wplanes_ref[0, 0, pair[0]], :, :192], jnp.concatenate([high, low, high], 0))
            for side, n in enumerate(pair):
                t = both[:, side * CH : (side + 1) * CH]
                vval, vblock = taps(1, n)
                are, aim = t[0:8], t[64:72]
                for j in range(1, 8):
                    here = vblock == j
                    are = jnp.where(here, t[8 * j : 8 * j + 8], are)
                    aim = jnp.where(here, t[64 + 8 * j : 72 + 8 * j], aim)
                place = packed[side] >> 9
                rows_ref[pl.ds(place, 1), :] = jnp.sum(are * vval, 0, keepdims=True)
                rows_ref[pl.ds(place + 8, 1), :] = jnp.sum(aim * vval, 0, keepdims=True)
        return carry

    lax.fori_loop(order_ref[ENDS + part], order_ref[ENDS + part + 1], body, 0)

    tiles = rows_ref[: 2 * CAP].reshape(CAP // 8, 2, 8, CH)
    out_ref[:, :CH] = tiles[:, 0].reshape(CAP, CH)
    out_ref[:, CH:] = tiles[:, 1].reshape(CAP, CH)


def degrid(part, order, wplanes, planes, offsets, frac):
    smem = pl.BlockSpec(memory_space=pltpu.SMEM)
    vmem = pl.BlockSpec(memory_space=pltpu.VMEM)
    return pl.pallas_call(
        functools.partial(degrid_kernel, part=part),
        in_specs=[smem] * 2 + [vmem] * 3,
        out_specs=vmem,
        out_shape=jax.ShapeDtypeStruct((CAP, 2 * CH), F32),
        scratch_shapes=[pltpu.VMEM((2 * CAP + 16, CH), F32)],
        compiler_params=pltpu.CompilerParams(vmem_limit_bytes=VMEM_LIMIT),
        cost_estimate=pl.CostEstimate(flops=2_500_000_000, bytes_accessed=2_000_000, transcendentals=0),
        name="degrid_" + ("cross", "chip", "core", "own")[part],
    )(order, wplanes, planes, offsets, frac)


def gather_kernel(self_ref, core_ref, chip_ref, cross_ref, out_ref, sems):
    vis = lax.axis_index("vis")
    copies = [
        pltpu.make_async_copy(ref, out_ref.at[0, 0, vis ^ i], sems.at[i])
        for i, ref in enumerate((self_ref, core_ref, chip_ref, cross_ref))
    ]
    for copy in copies:
        copy.start()
    for copy in copies:
        copy.wait()


def gather_rows(*blocks):
    return pl.pallas_call(
        gather_kernel,
        in_specs=[pl.BlockSpec(memory_space=pltpu.VMEM)] * N_VIS,
        out_specs=pl.BlockSpec(memory_space=pl.ANY),
        out_shape=jax.ShapeDtypeStruct((1, 1, N_VIS, CAP, 2 * CH), F32),
        scratch_shapes=[pltpu.SemaphoreType.DMA((N_VIS,))],
        compiler_params=pltpu.CompilerParams(vmem_limit_bytes=8 * 1024 * 1024),
        name="gather_rows",
    )(*blocks)


TO_CORE = [(0, 1), (1, 0), (2, 3), (3, 2)]
TO_CHIP = [(0, 2), (2, 0), (1, 3), (3, 1)]
TO_CROSS = [(0, 3), (3, 0), (1, 2), (2, 1)]


def on_device(facet_image, contributions, counts, wplanes, kernel_offsets, kernel_frac, owners):
    xtab, xrot, ytab, yrot, screens, left, right = [jnp.asarray(t) for t in tables()]
    parts = []
    for half in range(2):
        send, k0, k1 = x_sum(half, facet_image, xtab, xrot)
        received = lax.ppermute(send, "vis", TO_CORE)
        far = lax.ppermute(k0 + received[: 2 * SUB], "vis", TO_CHIP)
        parts.append((k1, received, far))
    blocks = y_sum(0, *parts[0], ytab, yrot)
    blocks = y_sum(1, *parts[1], ytab, yrot, blocks)
    order = order_rows(counts, wplanes, owners[..., 0])
    arrived = lax.all_to_all(blocks, "facet", split_axis=0, concat_axis=0, tiled=True)
    planes = make_planes(contributions[:, 0, :], arrived, screens, left, right)
    to_cross, to_chip, to_core, own = [
        degrid(part, order, wplanes, planes, kernel_offsets, kernel_frac) for part in range(N_VIS)
    ]
    from_cross = lax.ppermute(to_cross, "vis", TO_CROSS)
    from_chip = lax.ppermute(to_chip, "vis", TO_CHIP)
    to_core, from_cross = lax.optimization_barrier((to_core, from_cross))
    from_core = lax.ppermute(to_core, "vis", TO_CORE)
    return gather_rows(own, from_core, from_chip, from_cross)


def solution(mesh):
    return jax.shard_map(
        on_device,
        mesh=mesh,
        in_specs=(
            P(None, ("facet", "vis"), None),
            P(None, "facet", None),
            P("vis", "facet"),
            P("vis", "facet", None),
            P(None, "vis", "facet", None, None),
            P(None, "vis", "facet", None, None),
            P("vis", "facet", None, None),
        ),
        out_specs=P("vis", "facet", None, None, None),
        check_vma=False,
    )
```
